256 devices in a mesh: dp: 4 (over x), row: 4 (over z_lo), col: 16 (over z_hi, y, core).
Axes of the slice: x: 4, y: 4, z: 8 (z_hi: 2, z_lo: 4; z = z_hi * 4 + z_lo), core: 2. Of those that a mesh axis runs over, the one named last changes fastest.
Arguments:
- outer_gate: bfloat16 [4, 8, 1024, 1024], P('dp', None, ('row', 'col')), may hold values from -6 to 6
- inner_gate: bfloat16 [4, 8, 1024, 1024], P('dp', None, ('row', 'col')), may hold values from -6 to 6
- signal: bfloat16 [4, 8, 1024, 1024], P('dp', None, ('row', 'col')), may hold values from -6 to 6
- grad_out: bfloat16 [4, 8, 1024, 1024], P('dp', None, ('row', 'col')), may hold values from -6 to 6
- filter_weight: float32 [1024, 1024], P(('row', 'col')), may hold values from -6 to 6
Outputs:
- grad_outer: bfloat16 [4, 8, 1024, 1024], P('dp', None, ('row', 'col'))
- grad_inner: bfloat16 [4, 8, 1024, 1024], P('dp', None, ('row', 'col'))
- grad_signal: bfloat16 [4, 8, 1024, 1024], P('dp', None, ('row', 'col'))
- grad_filter: float32 [1024, 1024], P(('row', 'col'))
The draws below stay inside these ranges and needn't reach their ends.
All inputs are finite; a program needn't handle non-finite values.
Results may differ from the reference program's by a relative error of at most 0.0013.
Values sent between devices are 32-bit elements; how exact they have to be, the bound alone decides.
A program may use at most 128 MiB of HBM per device.

```python
import jax
import jax.numpy as jnp
from jax import lax

GRID = 1024
CH = 8
SEQS = 4


def level_of(own_key, extent, shards, least, high):
    def one(dim, blocks):
        heights = jax.random.uniform(jax.random.fold_in(jax.random.fold_in(own_key, 6), dim), (blocks,), jnp.float32, least / len(shards), high / len(shards))
        return jnp.repeat(jnp.exp(heights), extent[dim] // blocks).reshape((-1,) + (1,) * (len(extent) - dim - 1))

    factor_of = one(*shards[0])
    for cut in shards[1:]:
        factor_of = factor_of * one(*cut)
    return factor_of


def noise(stream_key, shape, scale, limit, shards=(), dtype=jnp.bfloat16):
    factor_of = level_of(stream_key, shape, shards, -0.22, 0.18) if shards else 1.0
    drawn = jax.random.normal(stream_key, shape, jnp.float32) * scale * factor_of
    return jnp.minimum(jnp.maximum(drawn, -limit), limit).astype(dtype)


def setup_inputs(seed: int = 0) -> dict:
    key_of = jax.random.split(jax.random.key(seed), 6)
    outer_gate = noise(key_of[0], (SEQS, CH, GRID, GRID), 1.0, 6.0, ((0, 4), (2, 64)))
    inner_gate = noise(key_of[1], (SEQS, CH, GRID, GRID), 1.0, 6.0, ((0, 4), (2, 64)))
    signal = noise(key_of[2], (SEQS, CH, GRID, GRID), 1.0, 6.0, ((0, 4), (2, 64)))
    grad_out = noise(key_of[3], (SEQS, CH, GRID, GRID), 1.0, 6.0, ((0, 4), (2, 64)))
    filter_weight = noise(key_of[4], (GRID, GRID), 1.0, 6.0, ((0, 64),), jnp.float32)
    return {"outer_gate": outer_gate, "inner_gate": inner_gate, "signal": signal, "grad_out": grad_out, "filter_weight": filter_weight}


def flatten_seq(array, seqs, total):
    return array.astype(jnp.float32).reshape(seqs, total)


def reference(outer_gate, inner_gate, signal, grad_out, filter_weight):
    total = GRID * GRID
    taps = filter_weight.astype(jnp.float32).reshape(total) * (1.0 / GRID)
    filt_spec = jnp.fft.fft(taps)

    def channel_grads(pieces):
        outer, inner, values, cotangent = pieces
        seqs = outer.shape[0]
        outer_f = flatten_seq(outer, seqs, total)
        inner_f = flatten_seq(inner, seqs, total)
        values_f = flatten_seq(values, seqs, total)
        grad_f = flatten_seq(cotangent, seqs, total)
        gated = inner_f * values_f
        gated_spec = jnp.fft.fft(gated, axis=-1)
        conv = jnp.real(jnp.fft.ifft(filt_spec[None, :] * gated_spec, axis=-1)).astype(jnp.float32)
        grad_outer = (grad_f * conv).astype(jnp.bfloat16)
        grad_conv = grad_f * outer_f
        conv_spec = jnp.fft.fft(grad_conv, axis=-1)
        grad_gated = jnp.real(jnp.fft.ifft(jnp.conj(filt_spec)[None, :] * conv_spec, axis=-1)).astype(jnp.float32)
        grad_inner = (grad_gated * values_f).astype(jnp.bfloat16)
        grad_signal = (grad_gated * inner_f).astype(jnp.bfloat16)
        filter_terms = jnp.real(jnp.fft.ifft(jnp.conj(gated_spec) * conv_spec, axis=-1)).astype(jnp.float32)
        shape = (seqs, GRID, GRID)
        return (grad_outer.reshape(shape), grad_inner.reshape(shape), grad_signal.reshape(shape),
                jnp.sum(filter_terms, axis=0).reshape(GRID, GRID))

    results = lax.map(channel_grads, (jnp.moveaxis(outer_gate, 1, 0), jnp.moveaxis(inner_gate, 1, 0),
                                      jnp.moveaxis(signal, 1, 0), jnp.moveaxis(grad_out, 1, 0)))
    grad_outer = jnp.moveaxis(results[0], 0, 1)
    grad_inner = jnp.moveaxis(results[1], 0, 1)
    grad_signal = jnp.moveaxis(results[2], 0, 1)
    grad_filter = jnp.sum(results[3], axis=0) * (1.0 / GRID)
    return grad_outer, grad_inner, grad_signal, grad_filter
```

```python
import functools
import math

import jax
import jax.numpy as jnp
import ml_dtypes
import numpy as np
from jax import lax
from jax.experimental import pallas as pl
from jax.experimental.pallas import tpu as pltpu
from jax.sharding import PartitionSpec as P

MESH = pl.DeviceIdType.MESH
F32 = jnp.float32
BF16 = jnp.bfloat16

SIDE = 1024
HALF = SIDE // 2
ROWS = 16
ZS = 8
SLABS = 8
LANES = SIDE // SLABS
KROWS = HALF // SLABS
RADIX = 4
QUARTER = SIDE // RADIX
PAD = KROWS + 8
ARRAYS = 3
KBLOCK = 2 * KROWS


def split_np(matrix):
    high = matrix.astype(np.float32).astype(ml_dtypes.bfloat16)
    low = (matrix - high.astype(np.float64)).astype(np.float32).astype(ml_dtypes.bfloat16)
    return np.stack([high, low])


def tables():
    side = np.arange(SIDE)
    half = np.arange(HALF)
    angle = 2 * np.pi * ((half[:, None] * side[None, :]) % SIDE) / SIDE
    cos, sin = np.cos(angle), np.sin(angle)
    sin[0] = (-1.0) ** side
    blocks = []
    for at in range(0, HALF, KBLOCK):
        blocks += [cos[at : at + KBLOCK], sin[at : at + KBLOCK]]
    rows_in = np.concatenate(blocks, axis=0)
    weight = np.where(half == 0, 0.5, 1.0)[:, None]
    rows_out = np.concatenate([cos * weight, -sin * weight], axis=0).T
    quarter = np.arange(QUARTER)
    small = 2 * np.pi * ((quarter[:, None] * quarter[None, :]) % QUARTER) / QUARTER
    cos_q, sin_q = np.cos(small), np.sin(small)
    cols_in = np.block([[cos_q, -sin_q], [sin_q, cos_q]])
    cols_out = np.block([[cos_q, sin_q], [-sin_q, cos_q]])
    total = SIDE * SIDE
    turn = 2 * np.pi * ((half[:, None] * side[None, :]) % total) / total
    turn = np.stack([np.cos(turn), np.sin(turn)]).reshape(2, HALF, SLABS, LANES)
    turn = np.transpose(turn, (2, 0, 1, 3)).astype(np.float32)
    twist = 2 * np.pi * np.arange(RADIX)[:, None] * quarter[None, :] / SIDE
    twist = np.concatenate([np.cos(twist), np.sin(twist)], axis=0).astype(np.float32)
    shift = np.pi * side / SIDE
    shift = np.stack([np.cos(shift), np.sin(shift)] * 4).astype(np.float32)
    return (
        split_np(rows_in),
        split_np(rows_out),
        split_np(cols_in),
        split_np(cols_out),
        turn,
        twist,
        shift,
    )


def split(value):
    high = value.astype(BF16)
    return high, (value - high.astype(F32)).astype(BF16)


def dot(left, right):
    return jnp.dot(left, right, preferred_element_type=F32)


def kernel(
    outer_ref, inner_ref, signal_ref, grad_ref, taps_ref, twist_ref, shift_ref,
    rows_in_hbm, rows_out_hbm, cols_in_hbm, cols_out_hbm, turn_hbm,
    d_outer_ref, d_inner_ref, d_signal_ref, d_taps_ref,
    rows_in, rows_out, cols_in, cols_out, turn,
    gated, cotangent, got_a, send_b, got_b, spec, send_c, got_c, done, got_d, part, got_e,
    halves, const_sem, send_sem, recv_sem,
):
    x = lax.axis_index("dp")
    row = lax.axis_index("row")
    col = lax.axis_index("col")
    rows_n = lax.axis_size("row")
    slab = lax.rem(col, SLABS)
    z = (col // SLABS) * rows_n + row
    block = row * lax.axis_size("col") + col

    def place(z_to, slab_to):
        return {"row": lax.rem(z_to, rows_n), "col": (z_to // rows_n) * SLABS + slab_to}

    consts = [
        pltpu.make_async_copy(source, target, const_sem.at[i])
        for i, (source, target) in enumerate(
            [
                (rows_in_hbm, rows_in),
                (turn_hbm.at[slab], turn),
                (cols_in_hbm, cols_in),
                (cols_out_hbm, cols_out),
                (rows_out_hbm, rows_out),
            ]
        )
    ]
    for copy in consts:
        copy.start()

    barrier = pltpu.get_barrier_semaphore()

    def partner(i):
        return lax.rem(z + i // SLABS, ZS), lax.rem(slab + lax.rem(i, SLABS), SLABS)

    def greet(i, carry):
        pl.semaphore_signal(barrier, inc=1, device_id=place(*partner(i)), device_id_type=MESH)
        return carry

    lax.fori_loop(1, ZS * SLABS, greet, 0)
    dps = lax.axis_size("dp")
    for i in range(1, dps):
        pl.semaphore_signal(
            barrier, inc=1, device_id={"dp": lax.rem(x + i, dps)}, device_id_type=MESH
        )

    gated[...] = inner_ref[...].astype(F32) * signal_ref[...].astype(F32)
    cotangent[...] = grad_ref[...].astype(F32) * outer_ref[...].astype(F32)
    pl.semaphore_wait(barrier, ZS * SLABS - 1 + dps - 1)

    def lane_slab(at):
        return pl.ds(pl.multiple_of(at * LANES, LANES), LANES)

    def row_block(at):
        return pl.ds(pl.multiple_of(at * ROWS, ROWS), ROWS)

    def k_rows(at):
        return pl.ds(pl.multiple_of(at * KROWS, KROWS), KROWS)

    def send_a(a, source_of):
        target = got_a.at[a, row_block(block)]
        pltpu.make_async_copy(source_of(z, slab), target, recv_sem.at[0, a]).start()

        def step(i, carry):
            z_to, slab_to = partner(i)
            pltpu.make_async_remote_copy(
                src_ref=source_of(z_to, slab_to), dst_ref=target,
                send_sem=send_sem.at[0, a], recv_sem=recv_sem.at[0, a],
                device_id=place(z_to, slab_to), device_id_type=MESH,
            ).start()
            return carry

        lax.fori_loop(1, ZS * SLABS, step, 0)

    send_a(0, lambda z_to, slab_to: taps_ref.at[:, lane_slab(slab_to)])
    send_a(1, lambda z_to, slab_to: gated.at[z_to, :, lane_slab(slab_to)])
    send_a(2, lambda z_to, slab_to: cotangent.at[z_to, :, lane_slab(slab_to)])

    def rows_forward(a):
        pltpu.make_async_copy(got_a.at[a], got_a.at[a], recv_sem.at[0, a]).wait()
        high, low = split(got_a[a])
        halves[:, :LANES] = high
        halves[:, LANES:] = low

        def step(i, carry):
            pair = lax.rem(slab // 2 + i, SLABS // 2)
            at = pl.ds(pl.multiple_of(pair * 2 * KBLOCK, 2 * KBLOCK), 2 * KBLOCK)
            wide = dot(rows_in[0, at], halves[...])
            both = wide[:, :LANES] + wide[:, LANES:] + dot(rows_in[1, at], halves[:, :LANES])
            even, odd = both[:KBLOCK], both[KBLOCK:]
            at = pl.ds(pl.multiple_of(pair * KBLOCK, KBLOCK), KBLOCK)
            cos, sin = turn[0, at], turn[1, at]
            real = even * cos - odd * sin
            imag = -(even * sin + odd * cos)
            for j in range(2):
                part_of = slice(j * KROWS, (j + 1) * KROWS)
                slab_to = pair * 2 + j
                send_b[a, slab_to, 0] = real[part_of]
                send_b[a, slab_to, 1] = imag[part_of]
                source = send_b.at[a, slab_to]
                target = got_b.at[a, :, pl.ds(0, KROWS), lane_slab(slab)]

                @pl.when(slab_to == slab)
                def _():
                    pltpu.make_async_copy(source, target, recv_sem.at[1, a]).start()

                @pl.when(slab_to != slab)
                def _():
                    pltpu.make_async_remote_copy(
                        src_ref=source, dst_ref=target,
                        send_sem=send_sem.at[1, a], recv_sem=recv_sem.at[1, a],
                        device_id=place(z, slab_to), device_id_type=MESH,
                    ).start()

            return carry

        lax.fori_loop(0, SLABS // 2, step, 0)

    first = slab == 0
    top = lax.broadcasted_iota(jnp.int32, (8, SIDE), 0) == 0

    def cols_forward(a):
        arrived = got_b.at[a, :, pl.ds(0, KROWS)]
        pltpu.make_async_copy(arrived, arrived, recv_sem.at[1, a]).wait()
        head = got_b[a, 1, 0:8]
        lone = jnp.broadcast_to(head[0:1], (8, SIDE))
        got_b[a, 0, KROWS:PAD] = -lone * shift_ref[0:1]
        got_b[a, 1, KROWS:PAD] = lone * shift_ref[1:2]
        got_b[a, 1, 0:8] = jnp.where(jnp.logical_and(top, first), 0.0, head)
        real = [got_b[a, 0, :, i * QUARTER : (i + 1) * QUARTER] for i in range(RADIX)]
        imag = [got_b[a, 1, :, i * QUARTER : (i + 1) * QUARTER] for i in range(RADIX)]
        sum_r, dif_r = real[0] + real[2], real[0] - real[2]
        sum_i, dif_i = imag[0] + imag[2], imag[0] - imag[2]
        sum_r2, dif_r2 = real[1] + real[3], real[1] - real[3]
        sum_i2, dif_i2 = imag[1] + imag[3], imag[1] - imag[3]
        mixed = [
            (sum_r + sum_r2, sum_i + sum_i2),
            (dif_r + dif_i2, dif_i - dif_r2),
            (sum_r - sum_r2, sum_i - sum_i2),
            (dif_r - dif_i2, dif_i + dif_r2),
        ]
        lines = []
        for m, (re, im) in enumerate(mixed):
            if m:
                cos, sin = twist_ref[m : m + 1], twist_ref[RADIX + m : RADIX + m + 1]
                re, im = re * cos + im * sin, im * cos - re * sin
            lines.append(jnp.concatenate([re, im], axis=1))
        high, low = split(jnp.concatenate(lines, axis=0))
        spec[a] = dot(high, cols_in[0]) + dot(low, cols_in[0]) + dot(high, cols_in[1])

    def cols_back(a, real, imag):
        high, low = split(jnp.concatenate([real, imag], axis=1))
        back = dot(high, cols_out[0]) + dot(low, cols_out[0]) + dot(high, cols_out[1])
        pieces = []
        for m in range(RADIX):
            re = back[m * PAD : (m + 1) * PAD, :QUARTER]
            im = back[m * PAD : (m + 1) * PAD, QUARTER:]
            if m:
                cos, sin = twist_ref[m : m + 1], twist_ref[RADIX + m : RADIX + m + 1]
                re, im = re * cos - im * sin, im * cos + re * sin
            pieces.append((re, im))
        (r0, i0), (r1, i1), (r2, i2), (r3, i3) = pieces
        sum_r, dif_r, sum_i, dif_i = r0 + r2, r0 - r2, i0 + i2, i0 - i2
        sum_r2, dif_r2, sum_i2, dif_i2 = r1 + r3, r1 - r3, i1 + i3, i1 - i3
        out_r = jnp.concatenate(
            [sum_r + sum_r2, dif_r - dif_i2, sum_r - sum_r2, dif_r + dif_i2], axis=1
        )
        out_i = jnp.concatenate(
            [sum_i + sum_i2, dif_i + dif_r2, sum_i - sum_i2, dif_i - dif_r2], axis=1
        )
        lone = out_i[KROWS : KROWS + 1] * shift_ref[1:2] - out_r[KROWS : KROWS + 1] * shift_ref[0:1]
        send_c[a, 0] = out_r[:KROWS]
        send_c[a, 1] = out_i[:KROWS]
        send_c[a, 1, 0:8] = jnp.where(jnp.logical_and(top, first), lone, out_i[0:8])
        target = got_c.at[a, :, k_rows(slab)]
        pltpu.make_async_copy(
            send_c.at[a, :, :, lane_slab(slab)], target, recv_sem.at[2, a]
        ).start()

        def step(i, carry):
            slab_to = lax.rem(slab + i, SLABS)
            pltpu.make_async_remote_copy(
                src_ref=send_c.at[a, :, :, lane_slab(slab_to)], dst_ref=target,
                send_sem=send_sem.at[2, a], recv_sem=recv_sem.at[2, a],
                device_id=place(z, slab_to), device_id_type=MESH,
            ).start()
            return carry

        lax.fori_loop(1, SLABS, step, 0)

    scale = 2.0 / (SIDE * SIDE * SIDE)

    def rows_back(a):
        pltpu.make_async_copy(got_c.at[a], got_c.at[a], recv_sem.at[2, a]).wait()
        real, imag = got_c[a, 0], got_c[a, 1]
        cos, sin = turn[0], turn[1]
        high, low = split(real * cos - imag * sin)
        halves[:HALF, :LANES] = high
        halves[:HALF, LANES:] = low
        high, low = split(imag * cos + real * sin)
        halves[HALF:, :LANES] = high
        halves[HALF:, LANES:] = low

        def step(i, carry):
            at = pl.ds(pl.multiple_of(i * 256, 256), 256)
            wide = dot(rows_out[0, at], halves[...])
            both = wide[:, :LANES] + wide[:, LANES:] + dot(rows_out[1, at], halves[:, :LANES])
            done[a, at] = both * scale
            return carry

        lax.fori_loop(0, SIDE // 256, step, 0)
        target = got_d.at[a, z, :, lane_slab(slab)]
        pltpu.make_async_copy(done.at[a, row_block(block)], target, recv_sem.at[3, a]).start()

        def send(i, carry):
            z_to, slab_to = partner(i)
            to = place(z_to, slab_to)
            pltpu.make_async_remote_copy(
                src_ref=done.at[a, row_block(to["row"] * lax.axis_size("col") + to["col"])],
                dst_ref=target,
                send_sem=send_sem.at[3, a], recv_sem=recv_sem.at[3, a],
                device_id=to, device_id_type=MESH,
            ).start()
            return carry

        lax.fori_loop(1, ZS * SLABS, send, 0)

    def halves_of(a):
        return spec[a, :, :QUARTER], spec[a, :, QUARTER:]

    consts[0].wait()
    consts[1].wait()
    rows_forward(0)
    rows_forward(1)
    consts[2].wait()
    cols_forward(0)
    cols_forward(1)
    consts[3].wait()
    hr, hi = halves_of(0)
    gr, gi = halves_of(1)
    cols_back(0, hr * gr - hi * gi, hr * gi + hi * gr)
    rows_forward(2)
    consts[4].wait()
    rows_back(0)
    cols_forward(2)
    hr, hi = halves_of(0)
    cr, ci = halves_of(2)
    cols_back(1, hr * cr + hi * ci, hr * ci - hi * cr)
    gr, gi = halves_of(1)
    cols_back(2, gr * cr + gi * ci, gr * ci - gi * cr)
    rows_back(1)
    rows_back(2)

    pltpu.make_async_copy(got_d.at[0], got_d.at[0], recv_sem.at[3, 0]).wait()
    d_outer_ref[...] = (grad_ref[...].astype(F32) * got_d[0]).astype(BF16)
    pltpu.make_async_copy(got_d.at[1], got_d.at[1], recv_sem.at[3, 1]).wait()
    d_inner_ref[...] = (got_d[1] * signal_ref[...].astype(F32)).astype(BF16)
    d_signal_ref[...] = (got_d[1] * inner_ref[...].astype(F32)).astype(BF16)
    pltpu.make_async_copy(got_d.at[2], got_d.at[2], recv_sem.at[3, 2]).wait()
    part[...] = jnp.sum(got_d[2], axis=0)
    for i in range(1, dps):
        pltpu.make_async_remote_copy(
            src_ref=part, dst_ref=got_e.at[i - 1],
            send_sem=send_sem.at[4, 0], recv_sem=recv_sem.at[4, 0],
            device_id={"dp": lax.rem(x + i, dps)}, device_id_type=MESH,
        ).start()
    pltpu.make_async_copy(got_e, got_e, recv_sem.at[4, 0]).wait()
    d_taps_ref[...] = part[...] + got_e[0] + got_e[1] + got_e[2]

    for a in range(ARRAYS):
        sent = [
            got_a.at[a, pl.ds(0, SIDE - ROWS)],
            got_b.at[a, :, pl.ds(0, KROWS), pl.ds(0, SIDE - LANES)],
            got_c.at[a, :, pl.ds(0, HALF - KROWS)],
            done.at[a, pl.ds(0, SIDE - ROWS)],
        ]
        for phase, ref in enumerate(sent):
            pltpu.make_async_copy(ref, ref, send_sem.at[phase, a]).wait()
    pltpu.make_async_copy(got_e, got_e, send_sem.at[4, 0]).wait()


def shards(consts, outer_gate, inner_gate, signal, grad_out, filter_weight):
    rows_in, rows_out, cols_in, cols_out, turn, twist, shift = consts
    shape = outer_gate.shape[1:]
    vmem = pl.BlockSpec(memory_space=pltpu.VMEM)
    anywhere = pl.BlockSpec(memory_space=pl.ANY)
    outs = pl.pallas_call(
        kernel,
        out_shape=[jax.ShapeDtypeStruct(shape, BF16)] * 3
        + [jax.ShapeDtypeStruct(filter_weight.shape, F32)],
        in_specs=[vmem] * 7 + [anywhere] * 5,
        out_specs=[vmem] * 4,
        scratch_shapes=[
            pltpu.VMEM(rows_in.shape, BF16),
            pltpu.VMEM(rows_out.shape, BF16),
            pltpu.VMEM(cols_in.shape, BF16),
            pltpu.VMEM(cols_out.shape, BF16),
            pltpu.VMEM((2, HALF, LANES), F32),
            pltpu.VMEM(shape, F32),
            pltpu.VMEM(shape, F32),
            pltpu.VMEM((ARRAYS, SIDE, LANES), F32),
            pltpu.VMEM((ARRAYS, SLABS, 2, KROWS, LANES), F32),
            pltpu.VMEM((ARRAYS, 2, PAD, SIDE), F32),
            pltpu.VMEM((ARRAYS, RADIX * PAD, 2 * QUARTER), F32),
            pltpu.VMEM((ARRAYS, 2, KROWS, SIDE), F32),
            pltpu.VMEM((ARRAYS, 2, HALF, LANES), F32),
            pltpu.VMEM((ARRAYS, SIDE, LANES), F32),
            pltpu.VMEM((ARRAYS, ZS, ROWS, SIDE), F32),
            pltpu.VMEM((ROWS, SIDE), F32),
            pltpu.VMEM((3, ROWS, SIDE), F32),
            pltpu.VMEM((SIDE, 2 * LANES), BF16),
            pltpu.SemaphoreType.DMA((5,)),
            pltpu.SemaphoreType.DMA((5, ARRAYS)),
            pltpu.SemaphoreType.DMA((5, ARRAYS)),
        ],
        compiler_params=pltpu.CompilerParams(
            collective_id=0, has_side_effects=True, vmem_limit_bytes=56 * 1024 * 1024
        ),
    )(
        outer_gate[0], inner_gate[0], signal[0], grad_out[0], filter_weight, twist, shift,
        rows_in, rows_out, cols_in, cols_out, turn,
    )
    return outs[0][None], outs[1][None], outs[2][None], outs[3]


def solution(mesh):
    placed = P("dp", None, ("row", "col"), None)
    grid = P(("row", "col"), None)
    consts = tuple(jnp.asarray(table) for table in tables())
    return jax.shard_map(
        functools.partial(shards, consts),
        mesh=mesh,
        in_specs=(placed, placed, placed, placed, grid),
        out_specs=(placed, placed, placed, grid),
        check_vma=False,
    )
```

```python
import functools
import math

import jax
import jax.numpy as jnp
import ml_dtypes
import numpy as np
from jax import lax
from jax.experimental import pallas as pl
from jax.experimental.pallas import tpu as pltpu
from jax.sharding import PartitionSpec as P

MESH = pl.DeviceIdType.MESH
F32 = jnp.float32
BF16 = jnp.bfloat16

SIDE = 1024
ROWS = 16
ZS = 8
SLABS = 8
CHIPS = 4
DPS = 4
LINES = SIDE // ZS
KROWS = LINES // 2
PIECE = KROWS // DPS
LANES = 128
RADIX = 4
QUARTER = SIDE // RADIX
CHUNKS = 4
WIDTH = SIDE // CHUNKS
EXTRA = 16
ROOT = math.sqrt(0.5)
SCALE = 2.0 / SIDE**3


def split_np(matrix):
    high = matrix.astype(np.float32).astype(ml_dtypes.bfloat16)
    low = (matrix - high.astype(np.float64)).astype(np.float32).astype(ml_dtypes.bfloat16)
    return np.stack([high, low])


def tables():
    step = np.arange(KROWS)
    lists = [np.concatenate([8 * step, 8 * step + 4])]
    lists += [8 * np.arange(LINES) + y for y in range(1, CHIPS)]
    line = np.arange(LINES)
    rows_in, rows_out, turn = [], [], []
    side = np.arange(SIDE)
    for y, k1 in enumerate(lists):
        angle = 2 * np.pi * ((k1[:, None] * line[None, :]) % SIDE) / SIDE
        cos, sin = np.cos(angle), np.sin(angle)
        weight = np.ones(2 * LINES)
        if y == 0:
            none = np.zeros((KROWS, LINES))
            sin[0] = (-1.0) ** line
            matrix = np.block(
                [[cos[:KROWS], none], [none, cos[KROWS:]], [-sin[:KROWS], none], [none, -sin[KROWS:]]]
            )
            weight[0] = weight[LINES] = 0.5
        else:
            matrix = np.block([[cos, sin], [-sin, cos]])
        rows_in.append(split_np(matrix))
        rows_out.append(split_np((matrix * weight[:, None]).T * SCALE))
        angle = 2 * np.pi * ((k1[:, None] * side[None, :]) % SIDE**2) / SIDE**2
        turn.append(np.stack([np.cos(angle), np.sin(angle)]).astype(np.float32))
    quarter = np.arange(QUARTER)
    small = 2 * np.pi * ((quarter[:, None] * quarter[None, :]) % QUARTER) / QUARTER
    cos, sin = np.cos(small), np.sin(small)
    cols_in = split_np(np.block([[cos, -sin], [sin, cos]]))
    cols_out = split_np(np.block([[cos, sin], [-sin, cos]]))
    twist = 2 * np.pi * np.arange(RADIX)[:, None] * quarter[None, :] / SIDE
    twist = np.concatenate([np.cos(twist), np.sin(twist)], axis=0).astype(np.float32)
    shift = np.pi * side / SIDE
    shift = np.stack([np.cos(shift), np.sin(shift)] * 4).astype(np.float32)
    return np.stack(rows_in), np.stack(rows_out), cols_in, cols_out, np.stack(turn), twist, shift


def split(value):
    high = value.astype(BF16)
    return high, (value - high.astype(F32)).astype(BF16)


def dot(left, right):
    return jnp.dot(left, right, preferred_element_type=F32)


def blocks_forward(x):
    e0, e1, e2, e3 = x[0] + x[4], x[1] + x[5], x[2] + x[6], x[3] + x[7]
    d0, d1, d2, d3 = x[0] - x[4], x[1] - x[5], x[2] - x[6], x[3] - x[7]
    even, odd = e0 + e2, e1 + e3
    less, more = ROOT * (d1 - d3), ROOT * (d1 + d3)
    return (
        even + odd, even - odd,
        d0 + less, -d2 - more,
        e0 - e2, e3 - e1,
        d0 - less, d2 - more,
    )


def blocks_back(u):
    u0, u4, a, b, c, d, e, f = u
    plus, minus = u0 + u4, u0 - u4
    even = (plus + c, minus - d, plus - c, minus + d)
    less, more = ROOT * (a - e), ROOT * (b + f)
    odd = (a + e, less - more, f - b, -less - more)
    return [even[i] + odd[i] for i in range(4)] + [even[i] - odd[i] for i in range(4)]


def kernel(
    outer_ref, inner_ref, signal_ref, grad_ref, taps_ref, twist_ref, shift_ref,
    rows_in_hbm, rows_out_hbm, cols_in_hbm, cols_out_hbm, turn_hbm,
    conv_ref, back_ref, d_taps_ref,
    rows_in, rows_out, cols_in, cols_out, turn, turn_f,
    gated, got_a, send_b, got_b, send_q, got_q, spec, spec_x, send_r, got_r, send_c, got_c, done, got_d,
    f1, f2s, f2, f3s, f3, f4s, f4xs, f4x, t4s, t4, t4xs, t4x, t3s, t3, t5s, t5, t2s, t2, t1s, t1,
    const_sem, send_sem, recv_sem,
):
    x = lax.axis_index("dp")
    row = lax.axis_index("row")
    col = lax.axis_index("col")
    slab = lax.rem(col, SLABS)
    zpos = (col // SLABS) * 4 + row
    zid = row * 2 + col // SLABS
    y = slab // 2
    core = lax.rem(slab, 2)
    mate = 1 - core

    def at_z(i):
        other = lax.rem(zpos + i, ZS)
        row_to, high = lax.rem(other, 4), other // 4
        return row_to * 2 + high, {"row": row_to, "col": high * SLABS + slab}

    def at_slab(slab_to):
        return {"col": (col // SLABS) * SLABS + slab_to}

    def wide(k):
        return pl.ds(pl.multiple_of(k * WIDTH, WIDTH), WIDTH)

    def lanes(k):
        return pl.ds(pl.multiple_of(k * LANES, LANES), LANES)

    def rows(k, count):
        return pl.ds(pl.multiple_of(k * count, count), count)

    consts = [
        pltpu.make_async_copy(source, target, const_sem.at[i])
        for i, (source, target) in enumerate(
            [
                (rows_in_hbm.at[y], rows_in),
                (turn_hbm.at[y, :, :, lanes(zid)], turn_f),
                (turn_hbm.at[y, :, :, wide(core)], turn.at[0]),
                (turn_hbm.at[y, :, :, wide(core + 2)], turn.at[1]),
                (cols_in_hbm, cols_in),
                (cols_out_hbm, cols_out),
                (rows_out_hbm.at[y], rows_out),
            ]
        )
    ]
    for copy in consts:
        copy.start()

    barrier = pltpu.get_barrier_semaphore()
    order = (4, 3, 5, 2, 6, 1, 7)
    partners = [at_z(i)[1] for i in order]
    partners += [at_slab(lax.rem(slab + i, SLABS)) for i in range(1, SLABS)]
    for i in range(1, DPS):
        to = lax.rem(x + i, DPS)
        partners += [{"dp": to}, {"dp": to, **at_slab(slab + 1 - 2 * core)}]
    for device in partners:
        pl.semaphore_signal(barrier, inc=1, device_id=device, device_id_type=MESH)
    gated[0] = inner_ref[...].astype(F32) * signal_ref[...].astype(F32)
    gated[1] = grad_ref[...].astype(F32) * outer_ref[...].astype(F32)
    pl.semaphore_wait(barrier, len(partners))

    names = {}

    def sem(name):
        return names.setdefault(name, len(names))

    for name in ["a", "c", "d"]:
        for k in range(2 * CHUNKS):
            sem((name, k))
    for name in ["b", "r"]:
        for k in range(4):
            sem((name, k))
    pending = []

    def push(source, target, index, device):
        pltpu.make_async_remote_copy(
            src_ref=source, dst_ref=target,
            send_sem=send_sem.at[index], recv_sem=recv_sem.at[index],
            device_id=device, device_id_type=MESH,
        ).start()

    def keep(source, target, index):
        pltpu.make_async_copy(source, target, recv_sem.at[index]).start()

    def await_all(ref, index):
        pltpu.make_async_copy(ref, ref, recv_sem.at[index]).wait()

    def sent(ref, index):
        pending.append((ref, index))

    def over_z(name, source_of, target):
        index = sem(name)
        keep(source_of(zid), target, index)
        for i in order:
            z_to, device = at_z(i)
            push(source_of(z_to), target, index, device)
        return index

    def send_a(a, k):
        at = pl.ds(k * WIDTH, WIDTH)
        index = over_z(
            ("a", a * CHUNKS + k), lambda z_to: gated.at[a, z_to, :, at], got_a.at[a, zid, :, at]
        )
        sent(got_a.at[a, pl.ds(0, ZS - 1), :, at], index)

    def send_bs(a, k):
        at = pl.ds(k * WIDTH, WIDTH)
        index = sem(("a", a * CHUNKS + k))
        await_all(got_a.at[a, :, :, at], index)
        units = blocks_forward([got_a[a, i, :, k * WIDTH : (k + 1) * WIDTH] for i in range(ZS)])
        for u, value in enumerate(units):
            send_b[a, u, :, k * WIDTH : (k + 1) * WIDTH] = value
        core_to, i = k % 2, k // 2
        index = sem(("b", a * 2 + i))
        target = got_b.at[a, i, :, rows(slab, ROWS)]
        for dy in range(CHIPS):
            y_to = lax.rem(y + dy, CHIPS)
            source = send_b.at[a, pl.ds(y_to * 2, 2), :, at]
            device = at_slab(y_to * 2 + core_to)
            if dy:
                push(source, target, index, device)
            else:
                @pl.when(core == core_to)
                def _():
                    keep(source, target, index)

                @pl.when(core != core_to)
                def _():
                    push(source, target, index, device)

    def rows_forward(a, i):
        await_all(got_b.at[a, i], sem(("b", a * 2 + i)))
        high, low = split(jnp.concatenate([got_b[a, i, 0], got_b[a, i, 1]], axis=0))
        both = dot(rows_in[0], high) + dot(rows_in[0], low) + dot(rows_in[1], high)
        re, im = both[:LINES], both[LINES:]
        cos, sin = turn[i, 0], turn[i, 1]
        send_q[a, i, 0] = re * cos + im * sin
        send_q[a, i, 1] = im * cos - re * sin
        index = sem(("q", a))
        target = got_q.at[a, :, :, wide(core + 2 * i)]
        keep(send_q.at[a, i, :, rows(core, KROWS)], target, index)
        push(send_q.at[a, i, :, rows(mate, KROWS)], target, index, at_slab(y * 2 + mate))

    first = slab == 0
    top = lax.broadcasted_iota(jnp.int32, (8, SIDE), 0) == 0
    line_8 = lax.broadcasted_iota(jnp.int32, (8, 2 * QUARTER), 0)

    def radix_in(real, imag):
        r = [real[:, i * QUARTER : (i + 1) * QUARTER] for i in range(RADIX)]
        m = [imag[:, i * QUARTER : (i + 1) * QUARTER] for i in range(RADIX)]
        sum_r, dif_r, sum_i, dif_i = r[0] + r[2], r[0] - r[2], m[0] + m[2], m[0] - m[2]
        sum_r2, dif_r2, sum_i2, dif_i2 = r[1] + r[3], r[1] - r[3], m[1] + m[3], m[1] - m[3]
        mixed = [
            (sum_r + sum_r2, sum_i + sum_i2),
            (dif_r + dif_i2, dif_i - dif_r2),
            (sum_r - sum_r2, sum_i - sum_i2),
            (dif_r - dif_i2, dif_i + dif_r2),
        ]
        parts = []
        for m, (re, im) in enumerate(mixed):
            if m:
                cos, sin = twist_ref[m : m + 1], twist_ref[RADIX + m : RADIX + m + 1]
                re, im = re * cos + im * sin, im * cos - re * sin
            parts.append(jnp.concatenate([re, im], axis=1))
        return parts

    def radix_out(parts):
        pieces = []
        for m, part in enumerate(parts):
            re, im = part[:, :QUARTER], part[:, QUARTER:]
            if m:
                cos, sin = twist_ref[m : m + 1], twist_ref[RADIX + m : RADIX + m + 1]
                re, im = re * cos - im * sin, im * cos + re * sin
            pieces.append((re, im))
        (r0, i0), (r1, i1), (r2, i2), (r3, i3) = pieces
        sum_r, dif_r, sum_i, dif_i = r0 + r2, r0 - r2, i0 + i2, i0 - i2
        sum_r2, dif_r2, sum_i2, dif_i2 = r1 + r3, r1 - r3, i1 + i3, i1 - i3
        out_r = jnp.concatenate(
            [sum_r + sum_r2, dif_r - dif_i2, sum_r - sum_r2, dif_r + dif_i2], axis=1
        )
        out_i = jnp.concatenate(
            [sum_i + sum_i2, dif_i + dif_r2, sum_i - sum_i2, dif_i - dif_r2], axis=1
        )
        return out_r, out_i

    def cols_forward(real, imag, special):
        head = imag[0:8]
        lone = head[0:1]
        extra = radix_in(-lone * shift_ref[0:1], lone * shift_ref[1:2])
        tail = jnp.zeros((8, 2 * QUARTER), F32)
        for m in range(RADIX):
            tail = jnp.where(line_8 == m, extra[m], tail)
        head = jnp.where(jnp.logical_and(top, special), 0.0, head)
        imag = jnp.concatenate([head, imag[8:]], axis=0)
        high, low = split(jnp.concatenate(radix_in(real, imag) + [tail, tail], axis=0))
        return dot(high, cols_in[0]) + dot(low, cols_in[0]) + dot(high, cols_in[1])

    def cols_back(parts, extra, special):
        count = parts.shape[1]
        stacked = jnp.concatenate([parts[m] for m in range(RADIX)] + [extra, extra], axis=0)
        high, low = split(stacked)
        back = dot(high, cols_out[0]) + dot(low, cols_out[0]) + dot(high, cols_out[1])
        tail = back[RADIX * count : RADIX * count + 8]
        lone_r, lone_i = radix_out([tail[m : m + 1] for m in range(RADIX)])
        lone = lone_i * shift_ref[1:2] - lone_r * shift_ref[0:1]
        out_r, out_i = radix_out([back[m * count : (m + 1) * count] for m in range(RADIX)])
        head = jnp.where(jnp.logical_and(top, special), lone, out_i[0:8])
        return out_r, jnp.concatenate([head, out_i[8:]], axis=0)

    def spectrum(a):
        await_all(got_q.at[a], sem(("q", a)))
        sent(send_q.at[a, :, :, pl.ds(0, KROWS)], sem(("q", a)))
        both = cols_forward(got_q[a, 0], got_q[a, 1], first)
        for m in range(RADIX):
            spec[a + 1, m] = both[m * KROWS : (m + 1) * KROWS]
        spec_x[a + 1] = both[RADIX * KROWS : RADIX * KROWS + 8]

    def times(left, right):
        lr, li = left[..., :QUARTER], left[..., QUARTER:]
        rr, ri = right[..., :QUARTER], right[..., QUARTER:]
        return jnp.concatenate([lr * rr - li * ri, lr * ri + li * rr], axis=-1)

    def conj_times(left, right):
        lr, li = left[..., :QUARTER], left[..., QUARTER:]
        rr, ri = right[..., :QUARTER], right[..., QUARTER:]
        return jnp.concatenate([lr * rr + li * ri, lr * ri - li * rr], axis=-1)

    def send_rs(a, parts, extra):
        out_r, out_i = cols_back(parts, extra, first)
        send_r[a, 0] = out_r
        send_r[a, 1] = out_i
        for i in range(2):
            index = sem(("r", a * 2 + i))
            target = got_r.at[a, i, :, rows(core, KROWS)]
            keep(send_r.at[a, :, :, wide(core + 2 * i)], target, index)
            push(send_r.at[a, :, :, wide(mate + 2 * i)], target, index, at_slab(y * 2 + mate))
            sent(got_r.at[a, i, :, pl.ds(0, KROWS)], index)

    def rows_back(a, i):
        await_all(got_r.at[a, i], sem(("r", a * 2 + i)))
        real, imag = got_r[a, i, 0], got_r[a, i, 1]
        cos, sin = turn[i, 0], turn[i, 1]
        high, low = split(
            jnp.concatenate([real * cos - imag * sin, imag * cos + real * sin], axis=0)
        )
        both = dot(rows_out[0], high) + dot(rows_out[0], low) + dot(rows_out[1], high)
        send_c[a, i, 0] = both[:LINES]
        send_c[a, i, 1] = both[LINES:]
        base = sem(("c", a * CHUNKS))
        k = core + 2 * i
        target = got_c.at[a, pl.ds(y * 2, 2), :, wide(k)]
        keep(send_c.at[a, i, :, rows(slab, ROWS)], target, base + k)
        for j in range(1, SLABS):
            slab_to = lax.rem(slab + j, SLABS)
            push(send_c.at[a, i, :, rows(slab_to, ROWS)], target, base + k, at_slab(slab_to))
        sent(send_c.at[a, i, :, pl.ds(0, (SLABS - 1) * ROWS)], base + k)

    def send_ds(a, k):
        at = pl.ds(k * WIDTH, WIDTH)
        await_all(got_c.at[a, :, :, at], sem(("c", a * CHUNKS + k)))
        out = blocks_back([got_c[a, u, :, k * WIDTH : (k + 1) * WIDTH] for u in range(8)])
        for i, value in enumerate(out):
            done[a, i, :, k * WIDTH : (k + 1) * WIDTH] = value
        index = over_z(
            ("d", a * CHUNKS + k), lambda z_to: done.at[a, z_to, :, at], got_d.at[a, zid, :, at]
        )
        sent(got_d.at[a, pl.ds(0, ZS - 1), :, at], index)

    index = over_z("f1", lambda z_to: taps_ref.at[:, lanes(z_to)], f1.at[zid])
    sent(f1.at[pl.ds(0, ZS - 1)], index)
    for k in range(3):
        send_a(0, k)

    await_all(f1, sem("f1"))
    for u, value in enumerate(blocks_forward([f1[i] for i in range(ZS)])):
        f2s[u] = value
    index = sem("f2")
    target = f2.at[:, rows(slab, ROWS)]
    keep(f2s.at[pl.ds(y * 2, 2)], target, index)
    for j in range(1, SLABS):
        slab_to = lax.rem(slab + j, SLABS)
        push(f2s.at[pl.ds((slab_to // 2) * 2, 2)], target, index, at_slab(slab_to))
    sent(f2.at[:, pl.ds(0, (SLABS - 1) * ROWS)], index)

    send_bs(0, 0)
    consts[0].wait()
    consts[1].wait()
    await_all(f2, sem("f2"))
    high, low = split(jnp.concatenate([f2[0], f2[1]], axis=0))
    mine = core * (KROWS // PIECE) + x
    halves = []
    for part in range(2):
        at = pl.ds(pl.multiple_of(part * LINES + mine * PIECE, PIECE), PIECE)
        halves.append(dot(rows_in[0, at], high) + dot(rows_in[0, at], low) + dot(rows_in[1, at], high))
    re, im = halves
    cos, sin = turn_f[0, rows(mine, PIECE)], turn_f[1, rows(mine, PIECE)]
    f3s[0] = re * cos + im * sin
    f3s[1] = im * cos - re * sin
    index = over_z("f3", lambda z_to: f3s, f3.at[:, :, lanes(zid)])
    sent(f3.at[:, :, pl.ds(0, SIDE - LANES)], index)

    send_a(0, 3)
    for k in range(CHUNKS):
        send_a(1, k)
    send_bs(0, 1)
    send_bs(0, 2)

    consts[4].wait()
    await_all(f3, sem("f3"))
    special = jnp.logical_and(first, x == 0)
    both = cols_forward(f3[0], f3[1], special)
    for m in range(RADIX):
        f4s[m] = both[m * PIECE : (m + 1) * PIECE]
    f4xs[...] = both[RADIX * PIECE : RADIX * PIECE + 8]
    index, index_x = sem("f4"), sem("f4x")
    target, target_x = spec.at[0, :, rows(x, PIECE)], f4x.at[x]
    keep(f4s, target, index)
    keep(f4xs, target_x, index_x)
    for i in (2, 1, 3):
        device = {"dp": lax.rem(x + i, DPS)}
        push(f4s, target, index, device)
        push(f4xs, target_x, index_x, device)
    sent(spec.at[0, :, pl.ds(0, (DPS - 1) * PIECE)], index)
    sent(f4x.at[pl.ds(0, DPS - 1)], index_x)

    consts[2].wait()
    consts[3].wait()
    send_bs(0, 3)
    rows_forward(0, 0)
    send_bs(1, 0)
    rows_forward(0, 1)
    spectrum(0)
    send_bs(1, 1)
    consts[5].wait()
    await_all(spec.at[0], sem("f4"))
    await_all(f4x, sem("f4x"))
    spec_x[0] = f4x[0]
    send_rs(0, times(spec[0], spec[1]), times(spec_x[0], spec_x[1]))
    send_bs(1, 2)
    consts[6].wait()
    rows_back(0, 0)
    rows_back(0, 1)
    rows_forward(1, 0)
    send_bs(1, 3)
    send_ds(0, 0)
    send_ds(0, 1)
    rows_forward(1, 1)
    send_ds(0, 2)
    send_ds(0, 3)
    spectrum(1)

    t4s[...] = conj_times(spec[1], spec[2])
    t4xs[...] = conj_times(spec_x[1], spec_x[2])
    index, index_x = sem("t4"), sem("t4x")
    keep(t4s.at[:, rows(x, PIECE)], t4.at[x], index)
    keep(t4xs, t4x.at[x], index_x)
    for i in (2, 1, 3):
        to = lax.rem(x + i, DPS)
        push(t4s.at[:, rows(to, PIECE)], t4.at[x], index, {"dp": to})
        push(t4xs, t4x.at[x], index_x, {"dp": to})
    sent(t4.at[pl.ds(0, DPS - 1)], index)
    sent(t4x.at[pl.ds(0, DPS - 1)], index_x)

    send_rs(1, conj_times(spec[0], spec[2]), conj_times(spec_x[0], spec_x[2]))
    rows_back(1, 0)
    rows_back(1, 1)

    await_all(t4, sem("t4"))
    await_all(t4x, sem("t4x"))
    out_r, out_i = cols_back(
        t4[0] + t4[1] + t4[2] + t4[3], t4x[0] + t4x[1] + t4x[2] + t4x[3], special
    )
    t3s[0] = out_r
    t3s[1] = out_i
    index = over_z("t3", lambda z_to: t3s.at[:, :, lanes(z_to)], t3.at[zid])
    sent(t3.at[pl.ds(0, ZS - 1)], index)
    send_ds(1, 0)
    send_ds(1, 1)

    await_all(t3, sem("t3"))
    t5s[...] = jnp.sum(t3[...], axis=0)
    index = sem("t5")
    target = t5.at[:, rows(mine, PIECE)]
    keep(t5s, target, index)
    push(t5s, target, index, at_slab(y * 2 + mate))
    for i in (2, 1, 3):
        to = lax.rem(x + i, DPS)
        push(t5s, target, index, {"dp": to})
        push(t5s, target, index, {"dp": to, **at_slab(y * 2 + mate)})
    sent(t5.at[:, pl.ds(0, LINES - PIECE)], index)
    send_ds(1, 2)
    send_ds(1, 3)

    await_all(t5, sem("t5"))
    real, imag = t5[0], t5[1]
    cos, sin = turn_f[0], turn_f[1]
    high, low = split(jnp.concatenate([real * cos - imag * sin, imag * cos + real * sin], axis=0))
    both = dot(rows_out[0], high) + dot(rows_out[0], low) + dot(rows_out[1], high)
    t2s[0] = both[:LINES]
    t2s[1] = both[LINES:]
    index = sem("t2")
    target = t2.at[pl.ds(y * 2, 2)]
    keep(t2s.at[:, rows(slab, ROWS)], target, index)
    for dy in (2, 1, 3):
        slab_to = lax.rem(y + dy, CHIPS) * 2 + core
        push(t2s.at[:, rows(slab_to, ROWS)], target, index, at_slab(slab_to))
    sent(t2.at[pl.ds(0, 2 * (CHIPS - 1))], index)

    await_all(t2, sem("t2"))
    for i, value in enumerate(blocks_back([t2[u] for u in range(8)])):
        t1s[i] = value
    index = over_z("t1", lambda z_to: t1s.at[z_to], t1.at[:, lanes(zid)])
    sent(t1.at[:, pl.ds(0, SIDE - LANES)], index)

    for a, ref in enumerate([conv_ref, back_ref]):
        for k in range(CHUNKS):
            await_all(got_d.at[a, :, :, pl.ds(k * WIDTH, WIDTH)], sem(("d", a * CHUNKS + k)))
        ref[...] = got_d[a]
    await_all(t1, sem("t1"))
    d_taps_ref[...] = t1[...]

    for ref, index in pending:
        pltpu.make_async_copy(ref, ref, send_sem.at[index]).wait()
    for a in range(2):
        for i in range(2):
            ref = got_b.at[a, i, :, pl.ds(0, (SLABS - 1) * ROWS)]
            pltpu.make_async_copy(ref, ref, send_sem.at[sem(("b", a * 2 + i))]).wait()


def finish(conv_ref, back_ref, taps_in, grad_ref, signal_ref, inner_ref, outer_out, inner_out, signal_out, taps_out):
    outer_out[...] = (grad_ref[...].astype(F32) * conv_ref[...]).astype(BF16)
    inner_out[...] = (back_ref[...] * signal_ref[...].astype(F32)).astype(BF16)
    signal_out[...] = (back_ref[...] * inner_ref[...].astype(F32)).astype(BF16)
    taps_out[...] = taps_in[...]


def shards(consts, outer_gate, inner_gate, signal, grad_out, filter_weight):
    rows_in, rows_out, cols_in, cols_out, turn, twist, shift = consts
    shape = outer_gate.shape[1:]
    vmem = pl.BlockSpec(memory_space=pltpu.VMEM)
    anywhere = pl.BlockSpec(memory_space=pl.ANY)
    floats = [
        (2, LINES, LANES),
        (2, ZS, ROWS, SIDE),
        (2, ZS, ROWS, SIDE),
        (2, 8, ROWS, SIDE),
        (2, 2, 2, LINES, WIDTH),
        (2, 2, 2, LINES, WIDTH),
        (2, 2, KROWS, SIDE),
        (3, RADIX, KROWS, 2 * QUARTER),
        (3, 8, 2 * QUARTER),
        (2, 2, KROWS, SIDE),
        (2, 2, 2, LINES, WIDTH),
        (2, 2, 2, LINES, WIDTH),
        (2, 8, ROWS, SIDE),
        (2, ZS, ROWS, SIDE),
        (2, ZS, ROWS, SIDE),
        (ZS, ROWS, LANES),
        (8, ROWS, LANES),
        (2, LINES, LANES),
        (2, PIECE, LANES),
        (2, PIECE, SIDE),
        (RADIX, PIECE, 2 * QUARTER),
        (8, 2 * QUARTER),
        (DPS, 8, 2 * QUARTER),
        (RADIX, KROWS, 2 * QUARTER),
        (DPS, RADIX, PIECE, 2 * QUARTER),
        (8, 2 * QUARTER),
        (DPS, 8, 2 * QUARTER),
        (2, PIECE, SIDE),
        (ZS, 2, PIECE, LANES),
        (2, PIECE, LANES),
        (2, LINES, LANES),
        (2, LINES, LANES),
        (8, ROWS, LANES),
        (ZS, ROWS, LANES),
        (ROWS, SIDE),
    ]
    conv, back, d_taps = pl.pallas_call(
        kernel,
        out_shape=[
            jax.ShapeDtypeStruct(shape, F32),
            jax.ShapeDtypeStruct(shape, F32),
            jax.ShapeDtypeStruct(filter_weight.shape, F32),
        ],
        in_specs=[vmem] * 7 + [anywhere] * 5,
        out_specs=[vmem] * 3,
        scratch_shapes=[
            pltpu.VMEM(rows_in.shape[1:], BF16),
            pltpu.VMEM(rows_out.shape[1:], BF16),
            pltpu.VMEM(cols_in.shape, BF16),
            pltpu.VMEM(cols_out.shape, BF16),
            pltpu.VMEM((2, 2, LINES, WIDTH), F32),
        ]
        + [pltpu.VMEM(size, F32) for size in floats]
        + [
            pltpu.SemaphoreType.DMA((7,)),
            pltpu.SemaphoreType.DMA((56,)),
            pltpu.SemaphoreType.DMA((56,)),
        ],
        compiler_params=pltpu.CompilerParams(
            collective_id=0, has_side_effects=True, vmem_limit_bytes=56 * 1024 * 1024
        ),
    )(
        outer_gate[0], inner_gate[0], signal[0], grad_out[0], filter_weight, twist, shift,
        rows_in, rows_out, cols_in, cols_out, turn,
    )
    outs = pl.pallas_call(
        finish,
        out_shape=[jax.ShapeDtypeStruct(shape, BF16)] * 3
        + [jax.ShapeDtypeStruct(filter_weight.shape, F32)],
        in_specs=[vmem] * 6,
        out_specs=[vmem] * 4,
    )(conv, back, d_taps, grad_out[0], signal[0], inner_gate[0])
    return outs[0][None], outs[1][None], outs[2][None], outs[3]


def solution(mesh):
    placed = P("dp", None, ("row", "col"), None)
    grid = P(("row", "col"), None)
    consts = tuple(jnp.asarray(table) for table in tables())
    return jax.shard_map(
        functools.partial(shards, consts),
        mesh=mesh,
        in_specs=(placed, placed, placed, placed, grid),
        out_specs=(placed, placed, placed, grid),
        check_vma=False,
    )
```

```python
import functools
import math

import jax
import jax.numpy as jnp
import ml_dtypes
import numpy as np
from jax import lax
from jax.experimental import pallas as pl
from jax.experimental.pallas import tpu as pltpu
from jax.sharding import PartitionSpec as P

MESH = pl.DeviceIdType.MESH
F32 = jnp.float32
BF16 = jnp.bfloat16

SIDE = 1024
ROWS = 16
ZS = 8
SLABS = 8
CHIPS = 4
DPS = 4
LINES = SIDE // ZS
KROWS = LINES // 2
RADIX = 4
QUARTER = SIDE // RADIX
CHUNKS = 4
WIDTH = SIDE // CHUNKS
ROOT = math.sqrt(0.5)
SCALE = 2.0 / SIDE**3


def split_np(matrix):
    high = matrix.astype(np.float32).astype(ml_dtypes.bfloat16)
    low = (matrix - high.astype(np.float64)).astype(np.float32).astype(ml_dtypes.bfloat16)
    return np.stack([high, low])


def tables():
    step = np.arange(KROWS)
    lists = [np.concatenate([8 * step, 8 * step + 4])]
    lists += [8 * np.arange(LINES) + y for y in range(1, CHIPS)]
    line = np.arange(LINES)
    rows_in, rows_out, turn = [], [], []
    side = np.arange(SIDE)
    for y, k1 in enumerate(lists):
        angle = 2 * np.pi * ((k1[:, None] * line[None, :]) % SIDE) / SIDE
        cos, sin = np.cos(angle), np.sin(angle)
        weight = np.ones(2 * LINES)
        if y == 0:
            none = np.zeros((KROWS, LINES))
            sin[0] = (-1.0) ** line
            matrix = np.block(
                [[cos[:KROWS], none], [none, cos[KROWS:]], [-sin[:KROWS], none], [none, -sin[KROWS:]]]
            )
            weight[0] = weight[LINES] = 0.5
        else:
            matrix = np.block([[cos, sin], [-sin, cos]])
        rows_in.append(split_np(matrix))
        rows_out.append(split_np((matrix * weight[:, None]).T * SCALE))
        angle = 2 * np.pi * ((k1[:, None] * side[None, :]) % SIDE**2) / SIDE**2
        turn.append(np.stack([np.cos(angle), np.sin(angle)]).astype(np.float32))
    quarter = np.arange(QUARTER)
    small = 2 * np.pi * ((quarter[:, None] * quarter[None, :]) % QUARTER) / QUARTER
    cos, sin = np.cos(small), np.sin(small)
    cols_in = split_np(np.block([[cos, -sin], [sin, cos]]))
    cols_out = split_np(np.block([[cos, sin], [-sin, cos]]))
    twist = 2 * np.pi * np.arange(RADIX)[:, None] * quarter[None, :] / SIDE
    twist = np.concatenate([np.cos(twist), np.sin(twist)], axis=0).astype(np.float32)
    shift = np.pi * side / SIDE
    shift = np.stack([np.cos(shift), np.sin(shift)] * 4).astype(np.float32)
    return np.stack(rows_in), np.stack(rows_out), cols_in, cols_out, np.stack(turn), twist, shift


def split(value):
    high = value.astype(BF16)
    return high, (value - high.astype(F32)).astype(BF16)


def dot(left, right):
    return jnp.dot(left, right, preferred_element_type=F32)


def blocks_forward(x):
    e0, e1, e2, e3 = x[0] + x[4], x[1] + x[5], x[2] + x[6], x[3] + x[7]
    d0, d1, d2, d3 = x[0] - x[4], x[1] - x[5], x[2] - x[6], x[3] - x[7]
    even, odd = e0 + e2, e1 + e3
    less, more = ROOT * (d1 - d3), ROOT * (d1 + d3)
    return (
        even + odd, even - odd,
        d0 + less, -d2 - more,
        e0 - e2, e3 - e1,
        d0 - less, d2 - more,
    )


def blocks_back(u):
    u0, u4, a, b, c, d, e, f = u
    plus, minus = u0 + u4, u0 - u4
    even = (plus + c, minus - d, plus - c, minus + d)
    less, more = ROOT * (a - e), ROOT * (b + f)
    odd = (a + e, less - more, f - b, -less - more)
    return [even[i] + odd[i] for i in range(4)] + [even[i] - odd[i] for i in range(4)]


def kernel(
    outer_hbm, inner_hbm, signal_hbm, grad_hbm, taps_hbm, twist_hbm, shift_hbm,
    rows_in_hbm, rows_out_hbm, cols_in_hbm, cols_out_hbm, turn_hbm,
    d_outer_ref, d_inner_ref, d_signal_ref, d_taps_ref,
    outer_ref, inner_ref, signal_ref, grad_ref, taps_ref, twist_ref, shift_ref,
    rows_in, rows_out, cols_in, cols_out, turn, turn_f,
    gated, got_a, send_b, got_b, send_q, got_q, spec, spec_x, send_r, got_r, send_c, got_c, done, got_d,
    f1, f2s, f2, f3s, t4s, t4, t2s, t2, t1s, t1, t0s, t0,
    input_sem, const_sem, send_sem, recv_sem,
):
    x = lax.axis_index("dp")
    row = lax.axis_index("row")
    col = lax.axis_index("col")
    slab = lax.rem(col, SLABS)
    zpos = (col // SLABS) * 4 + row
    zid = row * 2 + col // SLABS
    y = slab // 2
    core = lax.rem(slab, 2)
    mate = 1 - core

    def at_z(i):
        other = lax.rem(zpos + i, ZS)
        row_to, high = lax.rem(other, 4), other // 4
        return row_to * 2 + high, {"row": row_to, "col": high * SLABS + slab}

    def at_slab(slab_to):
        return {"col": (col // SLABS) * SLABS + slab_to}

    def wide(k):
        return pl.ds(pl.multiple_of(k * WIDTH, WIDTH), WIDTH)

    def rows(k, count):
        return pl.ds(pl.multiple_of(k * count, count), count)

    inputs = [
        pltpu.make_async_copy(source, target, input_sem.at[i])
        for i, (source, target) in enumerate(
            [
                (taps_hbm, taps_ref),
                (inner_hbm, inner_ref),
                (signal_hbm, signal_ref),
                (grad_hbm, grad_ref),
                (outer_hbm, outer_ref),
                (twist_hbm, twist_ref),
                (shift_hbm, shift_ref),
            ]
        )
    ]
    for copy in inputs:
        copy.start()

    barrier = pltpu.get_barrier_semaphore()
    order = (4, 3, 5, 2, 6, 1, 7)
    partners = [at_z(i)[1] for i in order]
    partners += [at_slab(lax.rem(slab + i, SLABS)) for i in range(1, SLABS)]
    for i in range(1, DPS):
        to = lax.rem(x + i, DPS)
        partners.append({"dp": to})
    for device in partners:
        pl.semaphore_signal(barrier, inc=1, device_id=device, device_id_type=MESH)
    consts = [
        pltpu.make_async_copy(source, target, const_sem.at[i])
        for i, (source, target) in enumerate(
            [
                (rows_in_hbm.at[y], rows_in),
                (turn_hbm.at[y, :, rows(core, KROWS), wide(x)], turn_f),
                (turn_hbm.at[y, :, :, wide(core)], turn.at[0]),
                (turn_hbm.at[y, :, :, wide(core + 2)], turn.at[1]),
                (cols_in_hbm, cols_in),
                (cols_out_hbm, cols_out),
                (rows_out_hbm.at[y], rows_out),
            ]
        )
    ]
    for copy in consts:
        copy.start()
    for copy in inputs:
        copy.wait()
    gated[0] = inner_ref[...].astype(F32) * signal_ref[...].astype(F32)
    gated[1] = grad_ref[...].astype(F32) * outer_ref[...].astype(F32)
    pl.semaphore_wait(barrier, len(partners))

    names = {}

    def sem(name):
        return names.setdefault(name, len(names))

    for name in ["a", "c", "d"]:
        for k in range(2 * CHUNKS):
            sem((name, k))
    for name in ["b", "r"]:
        for k in range(4):
            sem((name, k))
    pending = []

    def push(source, target, index, device):
        pltpu.make_async_remote_copy(
            src_ref=source, dst_ref=target,
            send_sem=send_sem.at[index], recv_sem=recv_sem.at[index],
            device_id=device, device_id_type=MESH,
        ).start()

    def keep(source, target, index):
        pltpu.make_async_copy(source, target, recv_sem.at[index]).start()

    def await_all(ref, index):
        pltpu.make_async_copy(ref, ref, recv_sem.at[index]).wait()

    def sent(ref, index):
        pending.append((ref, index))

    def over_z(name, source_of, target):
        index = sem(name)
        keep(source_of(zid), target, index)
        for i in order:
            z_to, device = at_z(i)
            push(source_of(z_to), target, index, device)
        return index

    def over_x(name, source_of, target):
        index = sem(name)
        keep(source_of(x), target, index)
        for i in (2, 1, 3):
            to = lax.rem(x + i, DPS)
            push(source_of(to), target, index, {"dp": to})
        return index

    def over_slabs(name, source_of, target):
        index = sem(name)
        keep(source_of(slab), target, index)
        for i in (4, 5, 3, 2, 6, 7, 1):
            slab_to = lax.rem(slab + i, SLABS)
            push(source_of(slab_to), target, index, at_slab(slab_to))
        return index

    def send_a(a, k):
        at = pl.ds(k * WIDTH, WIDTH)
        index = over_z(
            ("a", a * CHUNKS + k), lambda z_to: gated.at[a, z_to, :, at], got_a.at[a, zid, :, at]
        )
        sent(got_a.at[a, pl.ds(0, ZS - 1), :, at], index)

    def send_bs(a, k):
        at = pl.ds(k * WIDTH, WIDTH)
        index = sem(("a", a * CHUNKS + k))
        await_all(got_a.at[a, :, :, at], index)
        units = blocks_forward([got_a[a, i, :, k * WIDTH : (k + 1) * WIDTH] for i in range(ZS)])
        for u, value in enumerate(units):
            send_b[a, u, :, k * WIDTH : (k + 1) * WIDTH] = value
        core_to, i = k % 2, k // 2
        index = sem(("b", a * 2 + i))
        target = got_b.at[a, i, :, rows(slab, ROWS)]
        for dy in range(CHIPS):
            y_to = lax.rem(y + dy, CHIPS)
            source = send_b.at[a, pl.ds(y_to * 2, 2), :, at]
            device = at_slab(y_to * 2 + core_to)
            if dy:
                push(source, target, index, device)
            else:
                @pl.when(core == core_to)
                def _():
                    keep(source, target, index)

                @pl.when(core != core_to)
                def _():
                    push(source, target, index, device)

    def rows_forward(a, i):
        await_all(got_b.at[a, i], sem(("b", a * 2 + i)))
        high, low = split(jnp.concatenate([got_b[a, i, 0], got_b[a, i, 1]], axis=0))
        both = dot(rows_in[0], high) + dot(rows_in[0], low) + dot(rows_in[1], high)
        re, im = both[:LINES], both[LINES:]
        cos, sin = turn[i, 0], turn[i, 1]
        send_q[a, i, 0] = re * cos + im * sin
        send_q[a, i, 1] = im * cos - re * sin
        index = sem(("q", a + 1))
        target = got_q.at[a + 1, :, :, wide(core + 2 * i)]
        keep(send_q.at[a, i, :, rows(core, KROWS)], target, index)
        push(send_q.at[a, i, :, rows(mate, KROWS)], target, index, at_slab(y * 2 + mate))
        if i:
            sent(send_q.at[a, :, :, pl.ds(0, KROWS)], index)

    first = slab == 0
    top = lax.broadcasted_iota(jnp.int32, (8, SIDE), 0) == 0
    line_8 = lax.broadcasted_iota(jnp.int32, (8, 2 * QUARTER), 0)

    def radix_in(real, imag):
        r = [real[:, i * QUARTER : (i + 1) * QUARTER] for i in range(RADIX)]
        m = [imag[:, i * QUARTER : (i + 1) * QUARTER] for i in range(RADIX)]
        sum_r, dif_r, sum_i, dif_i = r[0] + r[2], r[0] - r[2], m[0] + m[2], m[0] - m[2]
        sum_r2, dif_r2, sum_i2, dif_i2 = r[1] + r[3], r[1] - r[3], m[1] + m[3], m[1] - m[3]
        mixed = [
            (sum_r + sum_r2, sum_i + sum_i2),
            (dif_r + dif_i2, dif_i - dif_r2),
            (sum_r - sum_r2, sum_i - sum_i2),
            (dif_r - dif_i2, dif_i + dif_r2),
        ]
        parts = []
        for m, (re, im) in enumerate(mixed):
            if m:
                cos, sin = twist_ref[m : m + 1], twist_ref[RADIX + m : RADIX + m + 1]
                re, im = re * cos + im * sin, im * cos - re * sin
            parts.append(jnp.concatenate([re, im], axis=1))
        return parts

    def radix_out(parts):
        pieces = []
        for m, part in enumerate(parts):
            re, im = part[:, :QUARTER], part[:, QUARTER:]
            if m:
                cos, sin = twist_ref[m : m + 1], twist_ref[RADIX + m : RADIX + m + 1]
                re, im = re * cos - im * sin, im * cos + re * sin
            pieces.append((re, im))
        (r0, i0), (r1, i1), (r2, i2), (r3, i3) = pieces
        sum_r, dif_r, sum_i, dif_i = r0 + r2, r0 - r2, i0 + i2, i0 - i2
        sum_r2, dif_r2, sum_i2, dif_i2 = r1 + r3, r1 - r3, i1 + i3, i1 - i3
        out_r = jnp.concatenate(
            [sum_r + sum_r2, dif_r - dif_i2, sum_r - sum_r2, dif_r + dif_i2], axis=1
        )
        out_i = jnp.concatenate(
            [sum_i + sum_i2, dif_i + dif_r2, sum_i - sum_i2, dif_i - dif_r2], axis=1
        )
        return out_r, out_i

    def cols_forward(real, imag, special):
        head = imag[0:8]
        lone = head[0:1]
        extra = radix_in(-lone * shift_ref[0:1], lone * shift_ref[1:2])
        tail = jnp.zeros((8, 2 * QUARTER), F32)
        for m in range(RADIX):
            tail = jnp.where(line_8 == m, extra[m], tail)
        head = jnp.where(jnp.logical_and(top, special), 0.0, head)
        imag = jnp.concatenate([head, imag[8:]], axis=0)
        high, low = split(jnp.concatenate(radix_in(real, imag) + [tail, tail], axis=0))
        return dot(high, cols_in[0]) + dot(low, cols_in[0]) + dot(high, cols_in[1])

    def cols_back(parts, extra, special):
        count = parts.shape[1]
        stacked = jnp.concatenate([parts[m] for m in range(RADIX)] + [extra, extra], axis=0)
        high, low = split(stacked)
        back = dot(high, cols_out[0]) + dot(low, cols_out[0]) + dot(high, cols_out[1])
        tail = back[RADIX * count : RADIX * count + 8]
        lone_r, lone_i = radix_out([tail[m : m + 1] for m in range(RADIX)])
        lone = lone_i * shift_ref[1:2] - lone_r * shift_ref[0:1]
        out_r, out_i = radix_out([back[m * count : (m + 1) * count] for m in range(RADIX)])
        head = jnp.where(jnp.logical_and(top, special), lone, out_i[0:8])
        return out_r, jnp.concatenate([head, out_i[8:]], axis=0)

    def spectrum(a):
        await_all(got_q.at[a], sem(("q", a)))
        both = cols_forward(got_q[a, 0], got_q[a, 1], first)
        for m in range(RADIX):
            spec[a, m] = both[m * KROWS : (m + 1) * KROWS]
        spec_x[a] = both[RADIX * KROWS : RADIX * KROWS + 8]

    def times(left, right):
        lr, li = left[..., :QUARTER], left[..., QUARTER:]
        rr, ri = right[..., :QUARTER], right[..., QUARTER:]
        return jnp.concatenate([lr * rr - li * ri, lr * ri + li * rr], axis=-1)

    def conj_times(left, right):
        lr, li = left[..., :QUARTER], left[..., QUARTER:]
        rr, ri = right[..., :QUARTER], right[..., QUARTER:]
        return jnp.concatenate([lr * rr + li * ri, lr * ri - li * rr], axis=-1)

    def send_rs(a, parts, extra):
        out_r, out_i = cols_back(parts, extra, first)
        send_r[a, 0] = out_r
        send_r[a, 1] = out_i
        for i in range(2):
            index = sem(("r", a * 2 + i))
            target = got_r.at[a, i, :, rows(core, KROWS)]
            keep(send_r.at[a, :, :, wide(core + 2 * i)], target, index)
            push(send_r.at[a, :, :, wide(mate + 2 * i)], target, index, at_slab(y * 2 + mate))
            sent(got_r.at[a, i, :, pl.ds(0, KROWS)], index)

    def rows_back(a, i):
        await_all(got_r.at[a, i], sem(("r", a * 2 + i)))
        real, imag = got_r[a, i, 0], got_r[a, i, 1]
        cos, sin = turn[i, 0], turn[i, 1]
        high, low = split(
            jnp.concatenate([real * cos - imag * sin, imag * cos + real * sin], axis=0)
        )
        both = dot(rows_out[0], high) + dot(rows_out[0], low) + dot(rows_out[1], high)
        send_c[a, i, 0] = both[:LINES]
        send_c[a, i, 1] = both[LINES:]
        base = sem(("c", a * CHUNKS))
        k = core + 2 * i
        target = got_c.at[a, pl.ds(y * 2, 2), :, wide(k)]
        keep(send_c.at[a, i, :, rows(slab, ROWS)], target, base + k)
        for j in range(1, SLABS):
            slab_to = lax.rem(slab + j, SLABS)
            push(send_c.at[a, i, :, rows(slab_to, ROWS)], target, base + k, at_slab(slab_to))
        sent(send_c.at[a, i, :, pl.ds(0, (SLABS - 1) * ROWS)], base + k)

    def send_ds(a, k):
        at = pl.ds(k * WIDTH, WIDTH)
        await_all(got_c.at[a, :, :, at], sem(("c", a * CHUNKS + k)))
        out = blocks_back([got_c[a, u, :, k * WIDTH : (k + 1) * WIDTH] for u in range(8)])
        for i, value in enumerate(out):
            done[a, i, :, k * WIDTH : (k + 1) * WIDTH] = value
        index = over_z(
            ("d", a * CHUNKS + k), lambda z_to: done.at[a, z_to, :, at], got_d.at[a, zid, :, at]
        )
        sent(got_d.at[a, pl.ds(0, ZS - 1), :, at], index)

    index = over_z("f1", lambda z_to: taps_ref.at[:, wide(x)], f1.at[zid])
    sent(f1.at[pl.ds(0, ZS - 1)], index)
    for k in range(CHUNKS):
        send_a(0, k)

    await_all(f1, sem("f1"))
    for u, value in enumerate(blocks_forward([f1[i] for i in range(ZS)])):
        f2s[u] = value
    index = over_slabs(
        "f2", lambda to: f2s.at[pl.ds((to // 2) * 2, 2)], f2.at[:, rows(slab, ROWS)]
    )
    sent(f2.at[:, pl.ds(0, (SLABS - 1) * ROWS)], index)

    consts[0].wait()
    consts[1].wait()
    await_all(f2, sem("f2"))
    high, low = split(jnp.concatenate([f2[0], f2[1]], axis=0))
    halves = []
    for part in range(2):
        at = pl.ds(pl.multiple_of(part * LINES + core * KROWS, KROWS), KROWS)
        halves.append(dot(rows_in[0, at], high) + dot(rows_in[0, at], low) + dot(rows_in[1, at], high))
    re, im = halves
    cos, sin = turn_f[0], turn_f[1]
    f3s[0] = re * cos + im * sin
    f3s[1] = im * cos - re * sin
    index = over_x(("q", 0), lambda to: f3s, got_q.at[0, :, :, wide(x)])
    sent(got_q.at[0, :, :, pl.ds(0, SIDE - WIDTH)], index)

    for k in range(CHUNKS):
        send_a(1, k)
    send_bs(0, 0)
    send_bs(0, 1)
    send_bs(0, 2)

    consts[2].wait()
    consts[3].wait()
    send_bs(0, 3)
    rows_forward(0, 0)
    send_bs(1, 0)
    consts[4].wait()
    spectrum(0)
    rows_forward(0, 1)
    spectrum(1)
    send_bs(1, 1)
    consts[5].wait()
    send_rs(0, times(spec[0], spec[1]), times(spec_x[0], spec_x[1]))
    send_bs(1, 2)
    consts[6].wait()
    rows_back(0, 0)
    rows_forward(1, 0)
    send_bs(1, 3)
    rows_back(0, 1)
    send_ds(0, 0)
    send_ds(0, 1)
    rows_forward(1, 1)
    spectrum(2)

    out_r, out_i = cols_back(conj_times(spec[1], spec[2]), conj_times(spec_x[1], spec_x[2]), first)
    t4s[0] = out_r
    t4s[1] = out_i
    index = over_x("t4", lambda to: t4s.at[:, :, wide(to)], t4.at[x])
    sent(t4.at[pl.ds(0, DPS - 1)], index)

    send_ds(0, 2)
    send_rs(1, conj_times(spec[0], spec[2]), conj_times(spec_x[0], spec_x[2]))
    send_ds(0, 3)
    rows_back(1, 0)
    rows_back(1, 1)
    send_ds(1, 0)

    send_ds(1, 1)
    await_all(t4, sem("t4"))
    real, imag = t4[0, 0] + t4[1, 0] + t4[2, 0] + t4[3, 0], t4[0, 1] + t4[1, 1] + t4[2, 1] + t4[3, 1]
    cos, sin = turn_f[0], turn_f[1]
    re, im = real * cos - imag * sin, imag * cos + real * sin
    low_half = core == 0
    stacked = [jnp.where(low_half, re, 0.0), jnp.where(low_half, 0.0, re)]
    stacked += [jnp.where(low_half, im, 0.0), jnp.where(low_half, 0.0, im)]
    high, low = split(jnp.concatenate(stacked, axis=0))
    both = dot(rows_out[0], high) + dot(rows_out[0], low) + dot(rows_out[1], high)
    t2s[0] = both[:LINES]
    t2s[1] = both[LINES:]
    index = over_slabs("t2", lambda to: t2s.at[:, rows(to, ROWS)], t2.at[core, pl.ds(y * 2, 2)])
    sent(t2s.at[:, pl.ds(0, (SLABS - 1) * ROWS)], index)
    await_all(t2, sem("t2"))
    for i, value in enumerate(blocks_back([t2[0, u] + t2[1, u] for u in range(8)])):
        t1s[i] = value
    index = over_z("t1", lambda z_to: t1s.at[z_to], t1.at[zid])
    sent(t1.at[pl.ds(0, ZS - 1)], index)
    send_ds(1, 2)
    send_ds(1, 3)
    await_all(t1, sem("t1"))
    t0s[...] = jnp.sum(t1[...], axis=0)
    index = over_x("t0", lambda to: t0s, t0.at[:, wide(x)])
    sent(t0.at[:, pl.ds(0, SIDE - WIDTH)], index)

    for k in range(CHUNKS):
        at = slice(k * WIDTH, (k + 1) * WIDTH)
        await_all(got_d.at[0, :, :, pl.ds(k * WIDTH, WIDTH)], sem(("d", k)))
        d_outer_ref[:, :, at] = (grad_ref[:, :, at].astype(F32) * got_d[0, :, :, at]).astype(BF16)
    for k in range(CHUNKS):
        at = slice(k * WIDTH, (k + 1) * WIDTH)
        await_all(got_d.at[1, :, :, pl.ds(k * WIDTH, WIDTH)], sem(("d", CHUNKS + k)))
        value = got_d[1, :, :, at]
        d_inner_ref[:, :, at] = (value * signal_ref[:, :, at].astype(F32)).astype(BF16)
        d_signal_ref[:, :, at] = (value * inner_ref[:, :, at].astype(F32)).astype(BF16)
    await_all(t0, sem("t0"))
    d_taps_ref[...] = t0[...]

    for ref, index in pending:
        pltpu.make_async_copy(ref, ref, send_sem.at[index]).wait()
    for a in range(2):
        for i in range(2):
            ref = got_b.at[a, i, :, pl.ds(0, (SLABS - 1) * ROWS)]
            pltpu.make_async_copy(ref, ref, send_sem.at[sem(("b", a * 2 + i))]).wait()


def finish(*refs):
    count = len(refs) // 2
    for i in range(count):
        refs[count + i][...] = refs[i][...]


def shards(consts, outer_gate, inner_gate, signal, grad_out, filter_weight):
    rows_in, rows_out, cols_in, cols_out, turn, twist, shift = consts
    shape = outer_gate.shape[1:]
    vmem = pl.BlockSpec(memory_space=pltpu.VMEM)
    anywhere = pl.BlockSpec(memory_space=pl.ANY)
    floats = [
        (2, KROWS, WIDTH),
        (2, ZS, ROWS, SIDE),
        (2, ZS, ROWS, SIDE),
        (2, 8, ROWS, SIDE),
        (2, 2, 2, LINES, WIDTH),
        (2, 2, 2, LINES, WIDTH),
        (3, 2, KROWS, SIDE),
        (3, RADIX, KROWS, 2 * QUARTER),
        (3, 8, 2 * QUARTER),
        (2, 2, KROWS, SIDE),
        (2, 2, 2, LINES, WIDTH),
        (2, 2, 2, LINES, WIDTH),
        (2, 8, ROWS, SIDE),
        (2, ZS, ROWS, SIDE),
        (2, ZS, ROWS, SIDE),
        (ZS, ROWS, WIDTH),
        (8, ROWS, WIDTH),
        (2, LINES, WIDTH),
        (2, KROWS, WIDTH),
        (2, KROWS, SIDE),
        (DPS, 2, KROWS, WIDTH),
        (2, LINES, WIDTH),
        (2, 8, ROWS, WIDTH),
        (ZS, ROWS, WIDTH),
        (ZS, ROWS, WIDTH),
        (ROWS, WIDTH),
        (ROWS, SIDE),
    ]
    results = [jax.ShapeDtypeStruct(shape, BF16)] * 3
    results += [jax.ShapeDtypeStruct(filter_weight.shape, F32)]
    outs = pl.pallas_call(
        kernel,
        out_shape=results,
        in_specs=[anywhere] * 12,
        out_specs=[vmem] * 4,
        scratch_shapes=[pltpu.VMEM(shape, BF16)] * 4
        + [pltpu.VMEM(filter_weight.shape, F32)]
        + [pltpu.VMEM(twist.shape, F32), pltpu.VMEM(shift.shape, F32)]
        + [
            pltpu.VMEM(rows_in.shape[1:], BF16),
            pltpu.VMEM(rows_out.shape[1:], BF16),
            pltpu.VMEM(cols_in.shape, BF16),
            pltpu.VMEM(cols_out.shape, BF16),
            pltpu.VMEM((2, 2, LINES, WIDTH), F32),
        ]
        + [pltpu.VMEM(size, F32) for size in floats]
        + [
            pltpu.SemaphoreType.DMA((7,)),
            pltpu.SemaphoreType.DMA((7,)),
            pltpu.SemaphoreType.DMA((56,)),
            pltpu.SemaphoreType.DMA((56,)),
        ],
        compiler_params=pltpu.CompilerParams(
            collective_id=0, has_side_effects=True, vmem_limit_bytes=56 * 1024 * 1024
        ),
    )(
        outer_gate[0], inner_gate[0], signal[0], grad_out[0], filter_weight, twist, shift,
        rows_in, rows_out, cols_in, cols_out, turn,
    )
    outs = pl.pallas_call(
        finish,
        out_shape=results,
        in_specs=[vmem] * 4,
        out_specs=[vmem] * 4,
    )(*outs)
    return outs[0][None], outs[1][None], outs[2][None], outs[3]


def solution(mesh):
    placed = P("dp", None, ("row", "col"), None)
    grid = P(("row", "col"), None)
    consts = tuple(jnp.asarray(table) for table in tables())
    return jax.shard_map(
        functools.partial(shards, consts),
        mesh=mesh,
        in_specs=(placed, placed, placed, placed, grid),
        out_specs=(placed, placed, placed, grid),
        check_vma=False,
    )
```

```python
import functools
import math

import jax
import jax.numpy as jnp
import ml_dtypes
import numpy as np
from jax import lax
from jax.experimental import pallas as pl
from jax.experimental.pallas import tpu as pltpu
from jax.sharding import PartitionSpec as P

MESH = pl.DeviceIdType.MESH
F32 = jnp.float32
BF16 = jnp.bfloat16

SIDE = 1024
ROWS = 16
ZS = 8
SLABS = 8
CHIPS = 4
DPS = 4
LINES = SIDE // ZS
KROWS = LINES // 2
RADIX = 4
QUARTER = SIDE // RADIX
CHUNKS = 4
WIDTH = SIDE // CHUNKS
ROOT = math.sqrt(0.5)
SCALE = 2.0 / SIDE**3


def split_np(matrix):
    high = matrix.astype(np.float32).astype(ml_dtypes.bfloat16)
    low = (matrix - high.astype(np.float64)).astype(np.float32).astype(ml_dtypes.bfloat16)
    return np.stack([high, low])


def tables():
    step = np.arange(KROWS)
    lists = [np.concatenate([8 * step, 8 * step + 4])]
    lists += [8 * np.arange(LINES) + y for y in range(1, CHIPS)]
    line = np.arange(LINES)
    rows_in, rows_out, turn = [], [], []
    side = np.arange(SIDE)
    for y, k1 in enumerate(lists):
        angle = 2 * np.pi * ((k1[:, None] * line[None, :]) % SIDE) / SIDE
        cos, sin = np.cos(angle), np.sin(angle)
        weight = np.ones(2 * LINES)
        if y == 0:
            none = np.zeros((KROWS, LINES))
            sin[0] = (-1.0) ** line
            matrix = np.block(
                [[cos[:KROWS], none], [none, cos[KROWS:]], [-sin[:KROWS], none], [none, -sin[KROWS:]]]
            )
            weight[0] = weight[LINES] = 0.5
        else:
            matrix = np.block([[cos, sin], [-sin, cos]])
        rows_in.append(split_np(matrix))
        rows_out.append(split_np((matrix * weight[:, None]).T * SCALE))
        angle = 2 * np.pi * ((k1[:, None] * side[None, :]) % SIDE**2) / SIDE**2
        turn.append(np.stack([np.cos(angle), np.sin(angle)]).astype(np.float32))
    quarter = np.arange(QUARTER)
    small = 2 * np.pi * ((quarter[:, None] * quarter[None, :]) % QUARTER) / QUARTER
    cos, sin = np.cos(small), np.sin(small)
    cols_in = split_np(np.block([[cos, -sin], [sin, cos]]))
    cols_out = split_np(np.block([[cos, sin], [-sin, cos]]))
    twist = 2 * np.pi * np.arange(RADIX)[:, None] * quarter[None, :] / SIDE
    twist = np.concatenate([np.cos(twist), np.sin(twist)], axis=0).astype(np.float32)
    shift = np.pi * side / SIDE
    shift = np.stack([np.cos(shift), np.sin(shift)] * 4).astype(np.float32)
    return np.stack(rows_in), np.stack(rows_out), cols_in, cols_out, np.stack(turn), twist, shift


def split(value):
    high = value.astype(BF16)
    return high, (value - high.astype(F32)).astype(BF16)


def dot(left, right):
    return jnp.dot(left, right, preferred_element_type=F32)


def blocks_forward(x):
    e0, e1, e2, e3 = x[0] + x[4], x[1] + x[5], x[2] + x[6], x[3] + x[7]
    d0, d1, d2, d3 = x[0] - x[4], x[1] - x[5], x[2] - x[6], x[3] - x[7]
    even, odd = e0 + e2, e1 + e3
    less, more = ROOT * (d1 - d3), ROOT * (d1 + d3)
    return (
        even + odd, even - odd,
        d0 + less, -d2 - more,
        e0 - e2, e3 - e1,
        d0 - less, d2 - more,
    )


def blocks_back(u):
    u0, u4, a, b, c, d, e, f = u
    plus, minus = u0 + u4, u0 - u4
    even = (plus + c, minus - d, plus - c, minus + d)
    less, more = ROOT * (a - e), ROOT * (b + f)
    odd = (a + e, less - more, f - b, -less - more)
    return [even[i] + odd[i] for i in range(4)] + [even[i] - odd[i] for i in range(4)]


def kernel(
    outer_hbm, inner_hbm, signal_hbm, grad_hbm, taps_hbm, twist_hbm, shift_hbm,
    rows_in_hbm, rows_out_hbm, cols_in_hbm, cols_out_hbm, turn_hbm,
    d_outer_ref, d_inner_ref, d_signal_ref, d_taps_ref,
    outer_ref, inner_ref, signal_ref, grad_ref, taps_ref, twist_ref, shift_ref,
    rows_in, rows_out, cols_in, cols_out, turn, turn_f,
    gated, got_a, send_b, got_b, send_q, got_q, spec, spec_x, send_r, got_r, send_c, got_c, done, got_d,
    f1, f2s, f2, f3s, t4s, t4, t2s, t2, t1s, t1, t0s, t0,
    input_sem, const_sem, send_sem, recv_sem,
):
    x = lax.axis_index("dp")
    row = lax.axis_index("row")
    col = lax.axis_index("col")
    slab = lax.rem(col, SLABS)
    zpos = (col // SLABS) * 4 + row
    zid = row * 2 + col // SLABS
    y = slab // 2
    core = lax.rem(slab, 2)
    mate = 1 - core

    def at_z(i):
        other = lax.rem(zpos + i, ZS)
        row_to, high = lax.rem(other, 4), other // 4
        return row_to * 2 + high, {"row": row_to, "col": high * SLABS + slab}

    def at_slab(slab_to):
        return {"col": (col // SLABS) * SLABS + slab_to}

    def wide(k):
        return pl.ds(pl.multiple_of(k * WIDTH, WIDTH), WIDTH)

    def rows(k, count):
        return pl.ds(pl.multiple_of(k * count, count), count)

    inputs = [
        pltpu.make_async_copy(source, target, input_sem.at[i])
        for i, (source, target) in enumerate(
            [
                (taps_hbm, taps_ref),
                (inner_hbm, inner_ref),
                (signal_hbm, signal_ref),
                (grad_hbm, grad_ref),
                (outer_hbm, outer_ref),
                (twist_hbm, twist_ref),
                (shift_hbm, shift_ref),
            ]
        )
    ]
    for copy in inputs:
        copy.start()

    barrier = pltpu.get_barrier_semaphore()
    order = (4, 5, 3, 6, 2, 7, 1)
    partners = [at_z(i)[1] for i in order]
    partners += [at_slab(lax.rem(slab + i, SLABS)) for i in range(1, SLABS)]
    for i in range(1, DPS):
        to = lax.rem(x + i, DPS)
        partners.append({"dp": to})
    for device in partners:
        pl.semaphore_signal(barrier, inc=1, device_id=device, device_id_type=MESH)
    consts = [
        pltpu.make_async_copy(source, target, const_sem.at[i])
        for i, (source, target) in enumerate(
            [
                (rows_in_hbm.at[y], rows_in),
                (turn_hbm.at[y, :, rows(core, KROWS), wide(x)], turn_f),
                (turn_hbm.at[y, :, :, wide(core)], turn.at[0]),
                (turn_hbm.at[y, :, :, wide(core + 2)], turn.at[1]),
                (cols_in_hbm, cols_in),
                (cols_out_hbm, cols_out),
                (rows_out_hbm.at[y], rows_out),
            ]
        )
    ]
    for copy in consts:
        copy.start()
    inputs[0].wait()
    pl.semaphore_wait(barrier, len(partners))

    names = {}

    def sem(name):
        return names.setdefault(name, len(names))

    for name in ["a", "c", "d"]:
        for k in range(2 * CHUNKS):
            sem((name, k))
    for name in ["b", "r"]:
        for k in range(4):
            sem((name, k))
    pending = []

    def push(source, target, index, device):
        pltpu.make_async_remote_copy(
            src_ref=source, dst_ref=target,
            send_sem=send_sem.at[index], recv_sem=recv_sem.at[index],
            device_id=device, device_id_type=MESH,
        ).start()

    def keep(source, target, index):
        pltpu.make_async_copy(source, target, recv_sem.at[index]).start()

    def await_all(ref, index):
        pltpu.make_async_copy(ref, ref, recv_sem.at[index]).wait()

    def sent(ref, index):
        pending.append((ref, index))

    def over_z(name, source_of, target):
        index = sem(name)
        keep(source_of(zid), target, index)
        for i in order:
            z_to, device = at_z(i)
            push(source_of(z_to), target, index, device)
        return index

    def over_x(name, source_of, target):
        index = sem(name)
        keep(source_of(x), target, index)
        for i in (2, 1, 3):
            to = lax.rem(x + i, DPS)
            push(source_of(to), target, index, {"dp": to})
        return index

    def over_slabs(name, source_of, target):
        index = sem(name)
        keep(source_of(slab), target, index)
        for i in (4, 5, 3, 2, 6, 7, 1):
            slab_to = lax.rem(slab + i, SLABS)
            push(source_of(slab_to), target, index, at_slab(slab_to))
        return index

    def send_a(a, k):
        left, right = [(inner_ref, signal_ref), (grad_ref, outer_ref)][a]
        at = slice(k * WIDTH, (k + 1) * WIDTH)
        gated[a, :, :, at] = left[:, :, at].astype(F32) * right[:, :, at].astype(F32)
        at = pl.ds(k * WIDTH, WIDTH)
        index = over_z(
            ("a", a * CHUNKS + k), lambda z_to: gated.at[a, z_to, :, at], got_a.at[a, zid, :, at]
        )
        sent(got_a.at[a, pl.ds(0, ZS - 1), :, at], index)

    def send_bs(a, k):
        at = pl.ds(k * WIDTH, WIDTH)
        index = sem(("a", a * CHUNKS + k))
        await_all(got_a.at[a, :, :, at], index)
        units = blocks_forward([got_a[a, i, :, k * WIDTH : (k + 1) * WIDTH] for i in range(ZS)])
        for u, value in enumerate(units):
            send_b[a, u, :, k * WIDTH : (k + 1) * WIDTH] = value
        core_to, i = k % 2, k // 2
        index = sem(("b", a * 2 + i))
        target = got_b.at[a, i, :, rows(slab, ROWS)]
        for dy in range(CHIPS):
            y_to = lax.rem(y + dy, CHIPS)
            source = send_b.at[a, pl.ds(y_to * 2, 2), :, at]
            device = at_slab(y_to * 2 + core_to)
            if dy:
                push(source, target, index, device)
            else:
                @pl.when(core == core_to)
                def _():
                    keep(source, target, index)

                @pl.when(core != core_to)
                def _():
                    push(source, target, index, device)

    def rows_forward(a, i):
        await_all(got_b.at[a, i], sem(("b", a * 2 + i)))
        high, low = split(jnp.concatenate([got_b[a, i, 0], got_b[a, i, 1]], axis=0))
        both = dot(rows_in[0], high) + dot(rows_in[0], low) + dot(rows_in[1], high)
        re, im = both[:LINES], both[LINES:]
        cos, sin = turn[i, 0], turn[i, 1]
        send_q[a, i, 0] = re * cos + im * sin
        send_q[a, i, 1] = im * cos - re * sin
        index = sem(("q", a + 1))
        target = got_q.at[a + 1, :, :, wide(core + 2 * i)]
        keep(send_q.at[a, i, :, rows(core, KROWS)], target, index)
        push(send_q.at[a, i, :, rows(mate, KROWS)], target, index, at_slab(y * 2 + mate))
        if i:
            sent(send_q.at[a, :, :, pl.ds(0, KROWS)], index)

    first = slab == 0
    top = lax.broadcasted_iota(jnp.int32, (8, SIDE), 0) == 0
    line_8 = lax.broadcasted_iota(jnp.int32, (8, 2 * QUARTER), 0)

    def radix_in(real, imag):
        r = [real[:, i * QUARTER : (i + 1) * QUARTER] for i in range(RADIX)]
        m = [imag[:, i * QUARTER : (i + 1) * QUARTER] for i in range(RADIX)]
        sum_r, dif_r, sum_i, dif_i = r[0] + r[2], r[0] - r[2], m[0] + m[2], m[0] - m[2]
        sum_r2, dif_r2, sum_i2, dif_i2 = r[1] + r[3], r[1] - r[3], m[1] + m[3], m[1] - m[3]
        mixed = [
            (sum_r + sum_r2, sum_i + sum_i2),
            (dif_r + dif_i2, dif_i - dif_r2),
            (sum_r - sum_r2, sum_i - sum_i2),
            (dif_r - dif_i2, dif_i + dif_r2),
        ]
        parts = []
        for m, (re, im) in enumerate(mixed):
            if m:
                cos, sin = twist_ref[m : m + 1], twist_ref[RADIX + m : RADIX + m + 1]
                re, im = re * cos + im * sin, im * cos - re * sin
            parts.append(jnp.concatenate([re, im], axis=1))
        return parts

    def radix_out(parts):
        pieces = []
        for m, part in enumerate(parts):
            re, im = part[:, :QUARTER], part[:, QUARTER:]
            if m:
                cos, sin = twist_ref[m : m + 1], twist_ref[RADIX + m : RADIX + m + 1]
                re, im = re * cos - im * sin, im * cos + re * sin
            pieces.append((re, im))
        (r0, i0), (r1, i1), (r2, i2), (r3, i3) = pieces
        sum_r, dif_r, sum_i, dif_i = r0 + r2, r0 - r2, i0 + i2, i0 - i2
        sum_r2, dif_r2, sum_i2, dif_i2 = r1 + r3, r1 - r3, i1 + i3, i1 - i3
        out_r = jnp.concatenate(
            [sum_r + sum_r2, dif_r - dif_i2, sum_r - sum_r2, dif_r + dif_i2], axis=1
        )
        out_i = jnp.concatenate(
            [sum_i + sum_i2, dif_i + dif_r2, sum_i - sum_i2, dif_i - dif_r2], axis=1
        )
        return out_r, out_i

    def cols_forward(real, imag, special):
        head = imag[0:8]
        lone = head[0:1]
        extra = radix_in(-lone * shift_ref[0:1], lone * shift_ref[1:2])
        tail = jnp.zeros((8, 2 * QUARTER), F32)
        for m in range(RADIX):
            tail = jnp.where(line_8 == m, extra[m], tail)
        head = jnp.where(jnp.logical_and(top, special), 0.0, head)
        imag = jnp.concatenate([head, imag[8:]], axis=0)
        high, low = split(jnp.concatenate(radix_in(real, imag) + [tail, tail], axis=0))
        return dot(high, cols_in[0]) + dot(low, cols_in[0]) + dot(high, cols_in[1])

    def cols_back(parts, extra, special):
        count = parts.shape[1]
        stacked = jnp.concatenate([parts[m] for m in range(RADIX)] + [extra, extra], axis=0)
        high, low = split(stacked)
        back = dot(high, cols_out[0]) + dot(low, cols_out[0]) + dot(high, cols_out[1])
        tail = back[RADIX * count : RADIX * count + 8]
        lone_r, lone_i = radix_out([tail[m : m + 1] for m in range(RADIX)])
        lone = lone_i * shift_ref[1:2] - lone_r * shift_ref[0:1]
        out_r, out_i = radix_out([back[m * count : (m + 1) * count] for m in range(RADIX)])
        head = jnp.where(jnp.logical_and(top, special), lone, out_i[0:8])
        return out_r, jnp.concatenate([head, out_i[8:]], axis=0)

    def spectrum(a):
        await_all(got_q.at[a], sem(("q", a)))
        both = cols_forward(got_q[a, 0], got_q[a, 1], first)
        for m in range(RADIX):
            spec[a, m] = both[m * KROWS : (m + 1) * KROWS]
        spec_x[a] = both[RADIX * KROWS : RADIX * KROWS + 8]

    def times(left, right):
        lr, li = left[..., :QUARTER], left[..., QUARTER:]
        rr, ri = right[..., :QUARTER], right[..., QUARTER:]
        return jnp.concatenate([lr * rr - li * ri, lr * ri + li * rr], axis=-1)

    def conj_times(left, right):
        lr, li = left[..., :QUARTER], left[..., QUARTER:]
        rr, ri = right[..., :QUARTER], right[..., QUARTER:]
        return jnp.concatenate([lr * rr + li * ri, lr * ri - li * rr], axis=-1)

    def send_rs(a, parts, extra):
        out_r, out_i = cols_back(parts, extra, first)
        send_r[a, 0] = out_r
        send_r[a, 1] = out_i
        for i in range(2):
            index = sem(("r", a * 2 + i))
            target = got_r.at[a, i, :, rows(core, KROWS)]
            keep(send_r.at[a, :, :, wide(core + 2 * i)], target, index)
            push(send_r.at[a, :, :, wide(mate + 2 * i)], target, index, at_slab(y * 2 + mate))
            sent(got_r.at[a, i, :, pl.ds(0, KROWS)], index)

    def rows_back(a, i):
        await_all(got_r.at[a, i], sem(("r", a * 2 + i)))
        real, imag = got_r[a, i, 0], got_r[a, i, 1]
        cos, sin = turn[i, 0], turn[i, 1]
        high, low = split(
            jnp.concatenate([real * cos - imag * sin, imag * cos + real * sin], axis=0)
        )
        both = dot(rows_out[0], high) + dot(rows_out[0], low) + dot(rows_out[1], high)
        send_c[a, i, 0] = both[:LINES]
        send_c[a, i, 1] = both[LINES:]
        base = sem(("c", a * CHUNKS))
        k = core + 2 * i
        target = got_c.at[a, pl.ds(y * 2, 2), :, wide(k)]
        keep(send_c.at[a, i, :, rows(slab, ROWS)], target, base + k)
        for j in range(1, SLABS):
            slab_to = lax.rem(slab + j, SLABS)
            push(send_c.at[a, i, :, rows(slab_to, ROWS)], target, base + k, at_slab(slab_to))
        sent(send_c.at[a, i, :, pl.ds(0, (SLABS - 1) * ROWS)], base + k)

    def send_ds(a, k):
        at = pl.ds(k * WIDTH, WIDTH)
        await_all(got_c.at[a, :, :, at], sem(("c", a * CHUNKS + k)))
        out = blocks_back([got_c[a, u, :, k * WIDTH : (k + 1) * WIDTH] for u in range(8)])
        for i, value in enumerate(out):
            done[a, i, :, k * WIDTH : (k + 1) * WIDTH] = value
        index = over_z(
            ("d", a * CHUNKS + k), lambda z_to: done.at[a, z_to, :, at], got_d.at[a, zid, :, at]
        )
        sent(got_d.at[a, pl.ds(0, ZS - 1), :, at], index)

    index = over_z("f1", lambda z_to: taps_ref.at[:, wide(x)], f1.at[zid])
    sent(f1.at[pl.ds(0, ZS - 1)], index)
    inputs[1].wait()
    inputs[2].wait()
    for k in range(CHUNKS):
        send_a(0, k)

    await_all(f1, sem("f1"))
    for u, value in enumerate(blocks_forward([f1[i] for i in range(ZS)])):
        f2s[u] = value
    index = over_slabs(
        "f2", lambda to: f2s.at[pl.ds((to // 2) * 2, 2)], f2.at[:, rows(slab, ROWS)]
    )
    sent(f2.at[:, pl.ds(0, (SLABS - 1) * ROWS)], index)

    consts[0].wait()
    consts[1].wait()
    await_all(f2, sem("f2"))
    high, low = split(jnp.concatenate([f2[0], f2[1]], axis=0))
    halves = []
    for part in range(2):
        at = pl.ds(pl.multiple_of(part * LINES + core * KROWS, KROWS), KROWS)
        halves.append(dot(rows_in[0, at], high) + dot(rows_in[0, at], low) + dot(rows_in[1, at], high))
    re, im = halves
    cos, sin = turn_f[0], turn_f[1]
    f3s[0] = re * cos + im * sin
    f3s[1] = im * cos - re * sin
    index = over_x(("q", 0), lambda to: f3s, got_q.at[0, :, :, wide(x)])
    sent(got_q.at[0, :, :, pl.ds(0, SIDE - WIDTH)], index)

    for copy in inputs[3:]:
        copy.wait()
    for k in range(CHUNKS):
        send_a(1, k)
    send_bs(0, 0)
    send_bs(0, 1)
    send_bs(0, 2)

    consts[2].wait()
    consts[3].wait()
    send_bs(0, 3)
    rows_forward(0, 0)
    send_bs(1, 0)
    consts[4].wait()
    spectrum(0)
    rows_forward(0, 1)
    send_bs(1, 1)
    spectrum(1)
    consts[5].wait()
    send_rs(0, times(spec[0], spec[1]), times(spec_x[0], spec_x[1]))
    send_bs(1, 2)
    consts[6].wait()
    rows_back(0, 0)
    rows_forward(1, 0)
    send_bs(1, 3)
    rows_back(0, 1)
    rows_forward(1, 1)
    send_ds(0, 0)
    send_ds(0, 1)
    spectrum(2)

    out_r, out_i = cols_back(conj_times(spec[1], spec[2]), conj_times(spec_x[1], spec_x[2]), first)
    t4s[0] = out_r
    t4s[1] = out_i
    index = over_x("t4", lambda to: t4s.at[:, :, wide(to)], t4.at[x])
    sent(t4.at[pl.ds(0, DPS - 1)], index)

    send_rs(1, conj_times(spec[0], spec[2]), conj_times(spec_x[0], spec_x[2]))
    send_ds(0, 2)
    rows_back(1, 0)
    send_ds(0, 3)
    rows_back(1, 1)
    send_ds(1, 0)
    await_all(t4, sem("t4"))
    real, imag = t4[0, 0] + t4[1, 0] + t4[2, 0] + t4[3, 0], t4[0, 1] + t4[1, 1] + t4[2, 1] + t4[3, 1]
    cos, sin = turn_f[0], turn_f[1]
    re, im = real * cos - imag * sin, imag * cos + real * sin
    low_half = core == 0
    stacked = [jnp.where(low_half, re, 0.0), jnp.where(low_half, 0.0, re)]
    stacked += [jnp.where(low_half, im, 0.0), jnp.where(low_half, 0.0, im)]
    high, low = split(jnp.concatenate(stacked, axis=0))
    both = dot(rows_out[0], high) + dot(rows_out[0], low) + dot(rows_out[1], high)
    t2s[0] = both[:LINES]
    t2s[1] = both[LINES:]
    index = over_slabs("t2", lambda to: t2s.at[:, rows(to, ROWS)], t2.at[core, pl.ds(y * 2, 2)])
    sent(t2s.at[:, pl.ds(0, (SLABS - 1) * ROWS)], index)
    send_ds(1, 1)
    await_all(t2, sem("t2"))
    for i, value in enumerate(blocks_back([t2[0, u] + t2[1, u] for u in range(8)])):
        t1s[i] = value
    index = over_z("t1", lambda z_to: t1s.at[z_to], t1.at[zid])
    sent(t1.at[pl.ds(0, ZS - 1)], index)
    send_ds(1, 2)
    send_ds(1, 3)
    await_all(t1, sem("t1"))
    t0s[...] = jnp.sum(t1[...], axis=0)
    index = over_x("t0", lambda to: t0s, t0.at[:, wide(x)])
    sent(t0.at[:, pl.ds(0, SIDE - WIDTH)], index)

    for k in range(CHUNKS):
        at = slice(k * WIDTH, (k + 1) * WIDTH)
        await_all(got_d.at[0, :, :, pl.ds(k * WIDTH, WIDTH)], sem(("d", k)))
        d_outer_ref[:, :, at] = (grad_ref[:, :, at].astype(F32) * got_d[0, :, :, at]).astype(BF16)
    for k in range(CHUNKS):
        at = slice(k * WIDTH, (k + 1) * WIDTH)
        await_all(got_d.at[1, :, :, pl.ds(k * WIDTH, WIDTH)], sem(("d", CHUNKS + k)))
        value = got_d[1, :, :, at]
        d_inner_ref[:, :, at] = (value * signal_ref[:, :, at].astype(F32)).astype(BF16)
        d_signal_ref[:, :, at] = (value * inner_ref[:, :, at].astype(F32)).astype(BF16)
    await_all(t0, sem("t0"))
    d_taps_ref[...] = t0[...]

    for ref, index in pending:
        pltpu.make_async_copy(ref, ref, send_sem.at[index]).wait()
    for a in range(2):
        for i in range(2):
            ref = got_b.at[a, i, :, pl.ds(0, (SLABS - 1) * ROWS)]
            pltpu.make_async_copy(ref, ref, send_sem.at[sem(("b", a * 2 + i))]).wait()


def finish(*refs):
    count = len(refs) // 2
    for i in range(count):
        refs[count + i][...] = refs[i][...]


def shards(consts, outer_gate, inner_gate, signal, grad_out, filter_weight):
    rows_in, rows_out, cols_in, cols_out, turn, twist, shift = consts
    shape = outer_gate.shape[1:]
    vmem = pl.BlockSpec(memory_space=pltpu.VMEM)
    anywhere = pl.BlockSpec(memory_space=pl.ANY)
    floats = [
        (2, KROWS, WIDTH),
        (2, ZS, ROWS, SIDE),
        (2, ZS, ROWS, SIDE),
        (2, 8, ROWS, SIDE),
        (2, 2, 2, LINES, WIDTH),
        (2, 2, 2, LINES, WIDTH),
        (3, 2, KROWS, SIDE),
        (3, RADIX, KROWS, 2 * QUARTER),
        (3, 8, 2 * QUARTER),
        (2, 2, KROWS, SIDE),
        (2, 2, 2, LINES, WIDTH),
        (2, 2, 2, LINES, WIDTH),
        (2, 8, ROWS, SIDE),
        (2, ZS, ROWS, SIDE),
        (2, ZS, ROWS, SIDE),
        (ZS, ROWS, WIDTH),
        (8, ROWS, WIDTH),
        (2, LINES, WIDTH),
        (2, KROWS, WIDTH),
        (2, KROWS, SIDE),
        (DPS, 2, KROWS, WIDTH),
        (2, LINES, WIDTH),
        (2, 8, ROWS, WIDTH),
        (ZS, ROWS, WIDTH),
        (ZS, ROWS, WIDTH),
        (ROWS, WIDTH),
        (ROWS, SIDE),
    ]
    results = [jax.ShapeDtypeStruct(shape, BF16)] * 3
    results += [jax.ShapeDtypeStruct(filter_weight.shape, F32)]
    outs = pl.pallas_call(
        kernel,
        out_shape=results,
        in_specs=[anywhere] * 12,
        out_specs=[vmem] * 4,
        scratch_shapes=[pltpu.VMEM(shape, BF16)] * 4
        + [pltpu.VMEM(filter_weight.shape, F32)]
        + [pltpu.VMEM(twist.shape, F32), pltpu.VMEM(shift.shape, F32)]
        + [
            pltpu.VMEM(rows_in.shape[1:], BF16),
            pltpu.VMEM(rows_out.shape[1:], BF16),
            pltpu.VMEM(cols_in.shape, BF16),
            pltpu.VMEM(cols_out.shape, BF16),
            pltpu.VMEM((2, 2, LINES, WIDTH), F32),
        ]
        + [pltpu.VMEM(size, F32) for size in floats]
        + [
            pltpu.SemaphoreType.DMA((7,)),
            pltpu.SemaphoreType.DMA((7,)),
            pltpu.SemaphoreType.DMA((56,)),
            pltpu.SemaphoreType.DMA((56,)),
        ],
        compiler_params=pltpu.CompilerParams(
            collective_id=0, has_side_effects=True, vmem_limit_bytes=56 * 1024 * 1024
        ),
    )(
        outer_gate[0], inner_gate[0], signal[0], grad_out[0], filter_weight, twist, shift,
        rows_in, rows_out, cols_in, cols_out, turn,
    )
    outs = pl.pallas_call(
        finish,
        out_shape=results,
        in_specs=[vmem] * 4,
        out_specs=[vmem] * 4,
    )(*outs)
    return outs[0][None], outs[1][None], outs[2][None], outs[3]


def solution(mesh):
    placed = P("dp", None, ("row", "col"), None)
    grid = P(("row", "col"), None)
    consts = tuple(jnp.asarray(table) for table in tables())
    return jax.shard_map(
        functools.partial(shards, consts),
        mesh=mesh,
        in_specs=(placed, placed, placed, placed, grid),
        out_specs=(placed, placed, placed, grid),
        check_vma=False,
    )
```

```python
import functools
import math

import jax
import jax.numpy as jnp
import ml_dtypes
import numpy as np
from jax import lax
from jax.experimental import pallas as pl
from jax.experimental.pallas import tpu as pltpu
from jax.sharding import PartitionSpec as P

MESH = pl.DeviceIdType.MESH
F32 = jnp.float32
BF16 = jnp.bfloat16

SIDE = 1024
ROWS = 16
ZS = 8
SLABS = 8
CHIPS = 4
DPS = 4
LINES = SIDE // ZS
KROWS = LINES // 2
RADIX = 4
QUARTER = SIDE // RADIX
CHUNKS = 4
WIDTH = SIDE // CHUNKS
ROOT = math.sqrt(0.5)
SCALE = 2.0 / SIDE**3


def split_np(matrix):
    high = matrix.astype(np.float32).astype(ml_dtypes.bfloat16)
    low = (matrix - high.astype(np.float64)).astype(np.float32).astype(ml_dtypes.bfloat16)
    return np.stack([high, low])


def tables():
    step = np.arange(KROWS)
    lists = [np.concatenate([8 * step, 8 * step + 4])]
    lists += [8 * np.arange(LINES) + y for y in range(1, CHIPS)]
    line = np.arange(LINES)
    rows_in, rows_out, turn = [], [], []
    side = np.arange(SIDE)
    for y, k1 in enumerate(lists):
        angle = 2 * np.pi * ((k1[:, None] * line[None, :]) % SIDE) / SIDE
        cos, sin = np.cos(angle), np.sin(angle)
        weight = np.ones(2 * LINES)
        if y == 0:
            none = np.zeros((KROWS, LINES))
            sin[0] = (-1.0) ** line
            matrix = np.block(
                [[cos[:KROWS], none], [none, cos[KROWS:]], [-sin[:KROWS], none], [none, -sin[KROWS:]]]
            )
            weight[0] = weight[LINES] = 0.5
        else:
            matrix = np.block([[cos, sin], [-sin, cos]])
        rows_in.append(split_np(matrix))
        rows_out.append(split_np((matrix * weight[:, None]).T * SCALE))
        angle = 2 * np.pi * ((k1[:, None] * side[None, :]) % SIDE**2) / SIDE**2
        turn.append(np.stack([np.cos(angle), np.sin(angle)]).astype(np.float32))
    quarter = np.arange(QUARTER)
    small = 2 * np.pi * ((quarter[:, None] * quarter[None, :]) % QUARTER) / QUARTER
    cos, sin = np.cos(small), np.sin(small)
    cols_in = split_np(np.block([[cos, -sin], [sin, cos]]))
    cols_out = split_np(np.block([[cos, sin], [-sin, cos]]))
    twist = 2 * np.pi * np.arange(RADIX)[:, None] * quarter[None, :] / SIDE
    twist = np.concatenate([np.cos(twist), np.sin(twist)], axis=0).astype(np.float32)
    shift = np.pi * side / SIDE
    shift = np.stack([np.cos(shift), np.sin(shift)] * 4).astype(np.float32)
    return np.stack(rows_in), np.stack(rows_out), cols_in, cols_out, np.stack(turn), twist, shift


def split(value):
    high = value.astype(BF16)
    return high, (value - high.astype(F32)).astype(BF16)


def dot(left, right):
    return jnp.dot(left, right, preferred_element_type=F32)


def blocks_forward(x):
    e0, e1, e2, e3 = x[0] + x[4], x[1] + x[5], x[2] + x[6], x[3] + x[7]
    d0, d1, d2, d3 = x[0] - x[4], x[1] - x[5], x[2] - x[6], x[3] - x[7]
    even, odd = e0 + e2, e1 + e3
    less, more = ROOT * (d1 - d3), ROOT * (d1 + d3)
    return (
        even + odd, even - odd,
        d0 + less, -d2 - more,
        e0 - e2, e3 - e1,
        d0 - less, d2 - more,
    )


def blocks_back(u):
    u0, u4, a, b, c, d, e, f = u
    plus, minus = u0 + u4, u0 - u4
    even = (plus + c, minus - d, plus - c, minus + d)
    less, more = ROOT * (a - e), ROOT * (b + f)
    odd = (a + e, less - more, f - b, -less - more)
    return [even[i] + odd[i] for i in range(4)] + [even[i] - odd[i] for i in range(4)]


def kernel(
    outer_hbm, inner_hbm, signal_hbm, grad_hbm, taps_hbm, twist_hbm, shift_hbm,
    rows_in_hbm, rows_out_hbm, cols_in_hbm, cols_out_hbm, turn_hbm,
    d_outer_hbm, d_inner_hbm, d_signal_hbm, d_taps_hbm,
    d_outer_ref, d_inner_ref, d_signal_ref,
    outer_ref, inner_ref, signal_ref, grad_ref, taps_ref, twist_ref, shift_ref,
    rows_in, rows_out, cols_in, cols_out, turn, turn_f,
    gated, got_a, send_b, got_b, send_q, got_q, spec, spec_x, send_r, got_r, send_c, got_c, done, got_d,
    f1, f2s, f2, f3s, t4s, t4, t2s, t2, t1s, t1, t0s, t0,
    input_sem, const_sem, out_sem, send_sem, recv_sem,
):
    x = lax.axis_index("dp")
    row = lax.axis_index("row")
    col = lax.axis_index("col")
    slab = lax.rem(col, SLABS)
    zpos = (col // SLABS) * 4 + row
    zid = row * 2 + col // SLABS
    y = slab // 2
    core = lax.rem(slab, 2)
    mate = 1 - core

    def at_z(i):
        other = lax.rem(zpos + i, ZS)
        row_to, high = lax.rem(other, 4), other // 4
        return row_to * 2 + high, {"row": row_to, "col": high * SLABS + slab}

    def at_slab(slab_to):
        return {"col": (col // SLABS) * SLABS + slab_to}

    def wide(k):
        return pl.ds(pl.multiple_of(k * WIDTH, WIDTH), WIDTH)

    def rows(k, count):
        return pl.ds(pl.multiple_of(k * count, count), count)

    inputs = [
        pltpu.make_async_copy(source, target, input_sem.at[i])
        for i, (source, target) in enumerate(
            [
                (taps_hbm, taps_ref),
                (inner_hbm, inner_ref),
                (signal_hbm, signal_ref),
                (grad_hbm, grad_ref),
                (outer_hbm, outer_ref),
                (twist_hbm, twist_ref),
                (shift_hbm, shift_ref),
            ]
        )
    ]
    for copy in inputs:
        copy.start()

    barrier = pltpu.get_barrier_semaphore()
    order = (4, 5, 3, 6, 2, 7, 1)
    partners = [at_z(i)[1] for i in order]
    partners += [at_slab(lax.rem(slab + i, SLABS)) for i in range(1, SLABS)]
    for i in range(1, DPS):
        to = lax.rem(x + i, DPS)
        partners.append({"dp": to})
    for device in partners:
        pl.semaphore_signal(barrier, inc=1, device_id=device, device_id_type=MESH)
    consts = [
        pltpu.make_async_copy(source, target, const_sem.at[i])
        for i, (source, target) in enumerate(
            [
                (rows_in_hbm.at[y], rows_in),
                (turn_hbm.at[y, :, rows(core, KROWS), wide(x)], turn_f),
                (turn_hbm.at[y, :, :, wide(core)], turn.at[0]),
                (turn_hbm.at[y, :, :, wide(core + 2)], turn.at[1]),
                (cols_in_hbm, cols_in),
                (cols_out_hbm, cols_out),
                (rows_out_hbm.at[y], rows_out),
            ]
        )
    ]
    for copy in consts:
        copy.start()
    inputs[0].wait()
    pl.semaphore_wait(barrier, len(partners))

    names = {}

    def sem(name):
        return names.setdefault(name, len(names))

    for name in ["a", "c", "d"]:
        for k in range(2 * CHUNKS):
            sem((name, k))
    for name in ["b", "r"]:
        for k in range(4):
            sem((name, k))
    pending = []

    def push(source, target, index, device):
        pltpu.make_async_remote_copy(
            src_ref=source, dst_ref=target,
            send_sem=send_sem.at[index], recv_sem=recv_sem.at[index],
            device_id=device, device_id_type=MESH,
        ).start()

    def keep(source, target, index):
        pltpu.make_async_copy(source, target, recv_sem.at[index]).start()

    def await_all(ref, index):
        pltpu.make_async_copy(ref, ref, recv_sem.at[index]).wait()

    def sent(ref, index):
        pending.append((ref, index))

    def over_z(name, source_of, target):
        index = sem(name)
        keep(source_of(zid), target, index)
        for i in order:
            z_to, device = at_z(i)
            push(source_of(z_to), target, index, device)
        return index

    def over_x(name, source_of, target):
        index = sem(name)
        keep(source_of(x), target, index)
        for i in (2, 1, 3):
            to = lax.rem(x + i, DPS)
            push(source_of(to), target, index, {"dp": to})
        return index

    def over_slabs(name, source_of, target):
        index = sem(name)
        keep(source_of(slab), target, index)
        for i in (4, 5, 3, 2, 6, 7, 1):
            slab_to = lax.rem(slab + i, SLABS)
            push(source_of(slab_to), target, index, at_slab(slab_to))
        return index

    def send_a(a, k):
        left, right = [(inner_ref, signal_ref), (grad_ref, outer_ref)][a]
        at = slice(k * WIDTH, (k + 1) * WIDTH)
        gated[a, :, :, at] = left[:, :, at].astype(F32) * right[:, :, at].astype(F32)
        at = pl.ds(k * WIDTH, WIDTH)
        index = over_z(
            ("a", a * CHUNKS + k), lambda z_to: gated.at[a, z_to, :, at], got_a.at[a, zid, :, at]
        )
        sent(got_a.at[a, pl.ds(0, ZS - 1), :, at], index)

    def send_bs(a, k):
        at = pl.ds(k * WIDTH, WIDTH)
        index = sem(("a", a * CHUNKS + k))
        await_all(got_a.at[a, :, :, at], index)
        units = blocks_forward([got_a[a, i, :, k * WIDTH : (k + 1) * WIDTH] for i in range(ZS)])
        for u, value in enumerate(units):
            send_b[a, u, :, k * WIDTH : (k + 1) * WIDTH] = value
        core_to, i = k % 2, k // 2
        index = sem(("b", a * 2 + i))
        target = got_b.at[a, i, :, rows(slab, ROWS)]
        for dy in range(CHIPS):
            y_to = lax.rem(y + dy, CHIPS)
            source = send_b.at[a, pl.ds(y_to * 2, 2), :, at]
            device = at_slab(y_to * 2 + core_to)
            if dy:
                push(source, target, index, device)
            else:
                @pl.when(core == core_to)
                def _():
                    keep(source, target, index)

                @pl.when(core != core_to)
                def _():
                    push(source, target, index, device)

    def rows_forward(a, i):
        await_all(got_b.at[a, i], sem(("b", a * 2 + i)))
        high, low = split(jnp.concatenate([got_b[a, i, 0], got_b[a, i, 1]], axis=0))
        both = dot(rows_in[0], high) + dot(rows_in[0], low) + dot(rows_in[1], high)
        re, im = both[:LINES], both[LINES:]
        cos, sin = turn[i, 0], turn[i, 1]
        send_q[a, i, 0] = re * cos + im * sin
        send_q[a, i, 1] = im * cos - re * sin
        index = sem(("q", a + 1))
        target = got_q.at[a + 1, :, :, wide(core + 2 * i)]
        keep(send_q.at[a, i, :, rows(core, KROWS)], target, index)
        push(send_q.at[a, i, :, rows(mate, KROWS)], target, index, at_slab(y * 2 + mate))
        if i:
            sent(send_q.at[a, :, :, pl.ds(0, KROWS)], index)

    first = slab == 0
    top = lax.broadcasted_iota(jnp.int32, (8, SIDE), 0) == 0
    line_8 = lax.broadcasted_iota(jnp.int32, (8, 2 * QUARTER), 0)

    def radix_in(real, imag):
        r = [real[:, i * QUARTER : (i + 1) * QUARTER] for i in range(RADIX)]
        m = [imag[:, i * QUARTER : (i + 1) * QUARTER] for i in range(RADIX)]
        sum_r, dif_r, sum_i, dif_i = r[0] + r[2], r[0] - r[2], m[0] + m[2], m[0] - m[2]
        sum_r2, dif_r2, sum_i2, dif_i2 = r[1] + r[3], r[1] - r[3], m[1] + m[3], m[1] - m[3]
        mixed = [
            (sum_r + sum_r2, sum_i + sum_i2),
            (dif_r + dif_i2, dif_i - dif_r2),
            (sum_r - sum_r2, sum_i - sum_i2),
            (dif_r - dif_i2, dif_i + dif_r2),
        ]
        parts = []
        for m, (re, im) in enumerate(mixed):
            if m:
                cos, sin = twist_ref[m : m + 1], twist_ref[RADIX + m : RADIX + m + 1]
                re, im = re * cos + im * sin, im * cos - re * sin
            parts.append(jnp.concatenate([re, im], axis=1))
        return parts

    def radix_out(parts):
        pieces = []
        for m, part in enumerate(parts):
            re, im = part[:, :QUARTER], part[:, QUARTER:]
            if m:
                cos, sin = twist_ref[m : m + 1], twist_ref[RADIX + m : RADIX + m + 1]
                re, im = re * cos - im * sin, im * cos + re * sin
            pieces.append((re, im))
        (r0, i0), (r1, i1), (r2, i2), (r3, i3) = pieces
        sum_r, dif_r, sum_i, dif_i = r0 + r2, r0 - r2, i0 + i2, i0 - i2
        sum_r2, dif_r2, sum_i2, dif_i2 = r1 + r3, r1 - r3, i1 + i3, i1 - i3
        out_r = jnp.concatenate(
            [sum_r + sum_r2, dif_r - dif_i2, sum_r - sum_r2, dif_r + dif_i2], axis=1
        )
        out_i = jnp.concatenate(
            [sum_i + sum_i2, dif_i + dif_r2, sum_i - sum_i2, dif_i - dif_r2], axis=1
        )
        return out_r, out_i

    def cols_forward(real, imag, special):
        head = imag[0:8]
        lone = head[0:1]
        extra = radix_in(-lone * shift_ref[0:1], lone * shift_ref[1:2])
        tail = jnp.zeros((8, 2 * QUARTER), F32)
        for m in range(RADIX):
            tail = jnp.where(line_8 == m, extra[m], tail)
        head = jnp.where(jnp.logical_and(top, special), 0.0, head)
        imag = jnp.concatenate([head, imag[8:]], axis=0)
        high, low = split(jnp.concatenate(radix_in(real, imag) + [tail, tail], axis=0))
        return dot(high, cols_in[0]) + dot(low, cols_in[0]) + dot(high, cols_in[1])

    def cols_back(parts, extra, special):
        count = parts.shape[1]
        stacked = jnp.concatenate([parts[m] for m in range(RADIX)] + [extra, extra], axis=0)
        high, low = split(stacked)
        back = dot(high, cols_out[0]) + dot(low, cols_out[0]) + dot(high, cols_out[1])
        tail = back[RADIX * count : RADIX * count + 8]
        lone_r, lone_i = radix_out([tail[m : m + 1] for m in range(RADIX)])
        lone = lone_i * shift_ref[1:2] - lone_r * shift_ref[0:1]
        out_r, out_i = radix_out([back[m * count : (m + 1) * count] for m in range(RADIX)])
        head = jnp.where(jnp.logical_and(top, special), lone, out_i[0:8])
        return out_r, jnp.concatenate([head, out_i[8:]], axis=0)

    def spectrum(a):
        await_all(got_q.at[a], sem(("q", a)))
        both = cols_forward(got_q[a, 0], got_q[a, 1], first)
        for m in range(RADIX):
            spec[a, m] = both[m * KROWS : (m + 1) * KROWS]
        spec_x[a] = both[RADIX * KROWS : RADIX * KROWS + 8]

    def times(left, right):
        lr, li = left[..., :QUARTER], left[..., QUARTER:]
        rr, ri = right[..., :QUARTER], right[..., QUARTER:]
        return jnp.concatenate([lr * rr - li * ri, lr * ri + li * rr], axis=-1)

    def conj_times(left, right):
        lr, li = left[..., :QUARTER], left[..., QUARTER:]
        rr, ri = right[..., :QUARTER], right[..., QUARTER:]
        return jnp.concatenate([lr * rr + li * ri, lr * ri - li * rr], axis=-1)

    def send_rs(a, parts, extra):
        out_r, out_i = cols_back(parts, extra, first)
        send_r[a, 0] = out_r
        send_r[a, 1] = out_i
        for i in range(2):
            index = sem(("r", a * 2 + i))
            target = got_r.at[a, i, :, rows(core, KROWS)]
            keep(send_r.at[a, :, :, wide(core + 2 * i)], target, index)
            push(send_r.at[a, :, :, wide(mate + 2 * i)], target, index, at_slab(y * 2 + mate))
            sent(got_r.at[a, i, :, pl.ds(0, KROWS)], index)

    def rows_back(a, i):
        await_all(got_r.at[a, i], sem(("r", a * 2 + i)))
        real, imag = got_r[a, i, 0], got_r[a, i, 1]
        cos, sin = turn[i, 0], turn[i, 1]
        high, low = split(
            jnp.concatenate([real * cos - imag * sin, imag * cos + real * sin], axis=0)
        )
        both = dot(rows_out[0], high) + dot(rows_out[0], low) + dot(rows_out[1], high)
        send_c[a, i, 0] = both[:LINES]
        send_c[a, i, 1] = both[LINES:]
        base = sem(("c", a * CHUNKS))
        k = core + 2 * i
        target = got_c.at[a, pl.ds(y * 2, 2), :, wide(k)]
        keep(send_c.at[a, i, :, rows(slab, ROWS)], target, base + k)
        for j in range(1, SLABS):
            slab_to = lax.rem(slab + j, SLABS)
            push(send_c.at[a, i, :, rows(slab_to, ROWS)], target, base + k, at_slab(slab_to))
        sent(send_c.at[a, i, :, pl.ds(0, (SLABS - 1) * ROWS)], base + k)

    def send_ds(a, k):
        at = pl.ds(k * WIDTH, WIDTH)
        await_all(got_c.at[a, :, :, at], sem(("c", a * CHUNKS + k)))
        out = blocks_back([got_c[a, u, :, k * WIDTH : (k + 1) * WIDTH] for u in range(8)])
        for i, value in enumerate(out):
            done[a, i, :, k * WIDTH : (k + 1) * WIDTH] = value
        index = over_z(
            ("d", a * CHUNKS + k), lambda z_to: done.at[a, z_to, :, at], got_d.at[a, zid, :, at]
        )
        sent(got_d.at[a, pl.ds(0, ZS - 1), :, at], index)

    index = over_z("f1", lambda z_to: taps_ref.at[:, wide(x)], f1.at[zid])
    sent(f1.at[pl.ds(0, ZS - 1)], index)
    inputs[1].wait()
    inputs[2].wait()
    for k in range(CHUNKS):
        send_a(0, k)

    await_all(f1, sem("f1"))
    for u, value in enumerate(blocks_forward([f1[i] for i in range(ZS)])):
        f2s[u] = value
    index = over_slabs(
        "f2", lambda to: f2s.at[pl.ds((to // 2) * 2, 2)], f2.at[:, rows(slab, ROWS)]
    )
    sent(f2.at[:, pl.ds(0, (SLABS - 1) * ROWS)], index)

    consts[0].wait()
    consts[1].wait()
    await_all(f2, sem("f2"))
    high, low = split(jnp.concatenate([f2[0], f2[1]], axis=0))
    halves = []
    for part in range(2):
        at = pl.ds(pl.multiple_of(part * LINES + core * KROWS, KROWS), KROWS)
        halves.append(dot(rows_in[0, at], high) + dot(rows_in[0, at], low) + dot(rows_in[1, at], high))
    re, im = halves
    cos, sin = turn_f[0], turn_f[1]
    f3s[0] = re * cos + im * sin
    f3s[1] = im * cos - re * sin
    index = over_x(("q", 0), lambda to: f3s, got_q.at[0, :, :, wide(x)])
    sent(got_q.at[0, :, :, pl.ds(0, SIDE - WIDTH)], index)

    for copy in inputs[3:]:
        copy.wait()
    for k in range(CHUNKS):
        send_a(1, k)
    send_bs(0, 0)
    send_bs(0, 1)
    send_bs(0, 2)

    consts[2].wait()
    consts[3].wait()
    send_bs(0, 3)
    rows_forward(0, 0)
    send_bs(1, 0)
    consts[4].wait()
    spectrum(0)
    rows_forward(0, 1)
    send_bs(1, 1)
    spectrum(1)
    consts[5].wait()
    send_rs(0, times(spec[0], spec[1]), times(spec_x[0], spec_x[1]))
    send_bs(1, 2)
    consts[6].wait()
    rows_back(0, 0)
    rows_forward(1, 0)
    send_bs(1, 3)
    rows_back(0, 1)
    rows_forward(1, 1)
    send_ds(0, 0)
    send_ds(0, 1)
    spectrum(2)

    out_r, out_i = cols_back(conj_times(spec[1], spec[2]), conj_times(spec_x[1], spec_x[2]), first)
    t4s[0] = out_r
    t4s[1] = out_i
    index = over_x("t4", lambda to: t4s.at[:, :, wide(to)], t4.at[x])
    sent(t4.at[pl.ds(0, DPS - 1)], index)

    send_rs(1, conj_times(spec[0], spec[2]), conj_times(spec_x[0], spec_x[2]))
    send_ds(0, 2)
    rows_back(1, 0)
    send_ds(0, 3)
    rows_back(1, 1)
    send_ds(1, 0)
    await_all(t4, sem("t4"))
    real, imag = t4[0, 0] + t4[1, 0] + t4[2, 0] + t4[3, 0], t4[0, 1] + t4[1, 1] + t4[2, 1] + t4[3, 1]
    cos, sin = turn_f[0], turn_f[1]
    re, im = real * cos - imag * sin, imag * cos + real * sin
    low_half = core == 0
    stacked = [jnp.where(low_half, re, 0.0), jnp.where(low_half, 0.0, re)]
    stacked += [jnp.where(low_half, im, 0.0), jnp.where(low_half, 0.0, im)]
    high, low = split(jnp.concatenate(stacked, axis=0))
    both = dot(rows_out[0], high) + dot(rows_out[0], low) + dot(rows_out[1], high)
    t2s[0] = both[:LINES]
    t2s[1] = both[LINES:]
    index = over_slabs("t2", lambda to: t2s.at[:, rows(to, ROWS)], t2.at[core, pl.ds(y * 2, 2)])
    sent(t2s.at[:, pl.ds(0, (SLABS - 1) * ROWS)], index)
    send_ds(1, 1)
    await_all(t2, sem("t2"))
    for i, value in enumerate(blocks_back([t2[0, u] + t2[1, u] for u in range(8)])):
        t1s[i] = value
    index = over_z("t1", lambda z_to: t1s.at[z_to], t1.at[zid])
    sent(t1.at[pl.ds(0, ZS - 1)], index)
    send_ds(1, 2)
    send_ds(1, 3)
    await_all(t1, sem("t1"))
    t0s[...] = jnp.sum(t1[...], axis=0)
    index = over_x("t0", lambda to: t0s, t0.at[:, wide(x)])
    sent(t0.at[:, pl.ds(0, SIDE - WIDTH)], index)

    written = []

    def write(source, target):
        copy = pltpu.make_async_copy(source, target, out_sem.at[len(written)])
        copy.start()
        written.append(copy)

    for k in range(CHUNKS):
        at = pl.ds(k * WIDTH, WIDTH)
        await_all(got_d.at[0, :, :, at], sem(("d", k)))
        d_outer_ref[:, :, at] = (grad_ref[:, :, at].astype(F32) * got_d[0, :, :, at]).astype(BF16)
    write(d_outer_ref, d_outer_hbm)
    for k in range(CHUNKS):
        at = pl.ds(k * WIDTH, WIDTH)
        await_all(got_d.at[1, :, :, at], sem(("d", CHUNKS + k)))
        value = got_d[1, :, :, at]
        d_inner_ref[:, :, at] = (value * signal_ref[:, :, at].astype(F32)).astype(BF16)
        d_signal_ref[:, :, at] = (value * inner_ref[:, :, at].astype(F32)).astype(BF16)
        write(d_inner_ref.at[:, :, at], d_inner_hbm.at[:, :, at])
        write(d_signal_ref.at[:, :, at], d_signal_hbm.at[:, :, at])
    await_all(t0, sem("t0"))
    write(t0, d_taps_hbm)

    for ref, index in pending:
        pltpu.make_async_copy(ref, ref, send_sem.at[index]).wait()
    for a in range(2):
        for i in range(2):
            ref = got_b.at[a, i, :, pl.ds(0, (SLABS - 1) * ROWS)]
            pltpu.make_async_copy(ref, ref, send_sem.at[sem(("b", a * 2 + i))]).wait()
    for copy in written:
        copy.wait()


def finish(*refs):
    count = len(refs) // 2
    for i in range(count):
        refs[count + i][...] = refs[i][...]


def shards(consts, outer_gate, inner_gate, signal, grad_out, filter_weight):
    rows_in, rows_out, cols_in, cols_out, turn, twist, shift = consts
    shape = outer_gate.shape[1:]
    vmem = pl.BlockSpec(memory_space=pltpu.VMEM)
    anywhere = pl.BlockSpec(memory_space=pl.ANY)
    floats = [
        (2, KROWS, WIDTH),
        (2, ZS, ROWS, SIDE),
        (2, ZS, ROWS, SIDE),
        (2, 8, ROWS, SIDE),
        (2, 2, 2, LINES, WIDTH),
        (2, 2, 2, LINES, WIDTH),
        (3, 2, KROWS, SIDE),
        (3, RADIX, KROWS, 2 * QUARTER),
        (3, 8, 2 * QUARTER),
        (2, 2, KROWS, SIDE),
        (2, 2, 2, LINES, WIDTH),
        (2, 2, 2, LINES, WIDTH),
        (2, 8, ROWS, SIDE),
        (2, ZS, ROWS, SIDE),
        (2, ZS, ROWS, SIDE),
        (ZS, ROWS, WIDTH),
        (8, ROWS, WIDTH),
        (2, LINES, WIDTH),
        (2, KROWS, WIDTH),
        (2, KROWS, SIDE),
        (DPS, 2, KROWS, WIDTH),
        (2, LINES, WIDTH),
        (2, 8, ROWS, WIDTH),
        (ZS, ROWS, WIDTH),
        (ZS, ROWS, WIDTH),
        (ROWS, WIDTH),
        (ROWS, SIDE),
    ]
    results = [jax.ShapeDtypeStruct(shape, BF16)] * 3
    results += [jax.ShapeDtypeStruct(filter_weight.shape, F32)]
    outs = pl.pallas_call(
        kernel,
        out_shape=results,
        in_specs=[anywhere] * 12,
        out_specs=[anywhere] * 4,
        scratch_shapes=[pltpu.VMEM(shape, BF16)] * 7
        + [pltpu.VMEM(filter_weight.shape, F32)]
        + [pltpu.VMEM(twist.shape, F32), pltpu.VMEM(shift.shape, F32)]
        + [
            pltpu.VMEM(rows_in.shape[1:], BF16),
            pltpu.VMEM(rows_out.shape[1:], BF16),
            pltpu.VMEM(cols_in.shape, BF16),
            pltpu.VMEM(cols_out.shape, BF16),
            pltpu.VMEM((2, 2, LINES, WIDTH), F32),
        ]
        + [pltpu.VMEM(size, F32) for size in floats]
        + [
            pltpu.SemaphoreType.DMA((7,)),
            pltpu.SemaphoreType.DMA((7,)),
            pltpu.SemaphoreType.DMA((2 + 2 * CHUNKS,)),
            pltpu.SemaphoreType.DMA((56,)),
            pltpu.SemaphoreType.DMA((56,)),
        ],
        compiler_params=pltpu.CompilerParams(
            collective_id=0, has_side_effects=True, vmem_limit_bytes=56 * 1024 * 1024
        ),
    )(
        outer_gate[0], inner_gate[0], signal[0], grad_out[0], filter_weight, twist, shift,
        rows_in, rows_out, cols_in, cols_out, turn,
    )
    outs = pl.pallas_call(
        finish,
        out_shape=results,
        in_specs=[vmem] * 4,
        out_specs=[vmem] * 4,
    )(*outs)
    return outs[0][None], outs[1][None], outs[2][None], outs[3]


def solution(mesh):
    placed = P("dp", None, ("row", "col"), None)
    grid = P(("row", "col"), None)
    consts = tuple(jnp.asarray(table) for table in tables())
    return jax.shard_map(
        functools.partial(shards, consts),
        mesh=mesh,
        in_specs=(placed, placed, placed, placed, grid),
        out_specs=(placed, placed, placed, grid),
        check_vma=False,
    )
```
